512 devices in a mesh: slab: 64 (over z, x), col: 8 (over y, core).
Axes of the slice: x: 4, y: 4, z: 16, core: 2. Of those that a mesh axis runs over, the one named last changes fastest.
Arguments:
- rhs: float32 [64, 262144], P(None, ('slab', 'col')), may hold values from -6 to 6
- start: float32 [64, 262144], P(None, ('slab', 'col')), may hold values from -4 to 4
- screen: float32 [64, 262144], P(None, ('slab', 'col')), may hold values from 0.2 to 5
- neighbours: int32 [27, 262144], P(None, ('slab', 'col')), may hold values from 0 to 1088, as said below
- col_send: int32 [2, 65536], P(None, ('slab', 'col')), may hold values from 0 to 512, as said below
- slab_send: int32 [2, 81920], P(None, ('slab', 'col')), may hold values from 0 to 768
- coarse_map: int32 [262144], P(('slab', 'col')), may hold values from 0 to 15
- coupling: float32 [128, 16, 4], P('slab', 'col'), may hold values from 0.1 to 1
- coarse_scale: float32 [128, 16, 4], P('slab', 'col'), may hold values from 0.05 to 0.2
Outputs:
- solution: float32 [64, 262144], P(None, ('slab', 'col'))
The draws below stay inside these ranges and needn't reach their ends.
Inputs may be any that keep to these rules, and one draw needn't show every extreme that they name: `neighbours`: indices into the extended brick list; index 512 is the zero brick, and offsets that leave the strip's height point to it. `col_send`: each block holds exactly 512 occupied bricks, in the order of their positions; its eight corner positions are always occupied.
All inputs are finite; a program needn't handle non-finite values.
Results may differ from the reference program's by a relative error of at most 0.0003.
Values sent between devices are 32-bit elements; how exact they have to be, the bound alone decides.
A program may use at most 64 MiB of HBM per device.

```python
import math
import jax
import jax.numpy as jnp
import numpy as np
from jax import lax

BX = 8
BY = 8
BZ = 16
SWEEPS = 2
NB = 512
FCOL = 128
FSLAB = 160
EXT = 1089
CX = 2
CY = 2
CZ = 4
CELLS = 16
LUMPED_BOXES = 128
NCY = 16
N_SLAB = 64
N_COL = 8


def brick_geometry(key):
    positions = BX * BY * BZ
    ar_pos = jnp.arange(positions, dtype=jnp.int32)
    pos_x = ar_pos // (BY * BZ)
    pos_y = ar_pos // BZ % BY
    pos_z = ar_pos % BZ
    corner = ((pos_x == 0) | (pos_x == BX - 1)) & ((pos_y == 0) | (pos_y == BY - 1)) & ((pos_z == 0) | (pos_z == BZ - 1))
    vacant = (pos_x == 0) & (pos_y == 0) & (pos_z == 1)
    topmost = (1 << 30) // positions - 4
    noise = jax.random.randint(jax.random.fold_in(key, 7), (N_SLAB, N_COL, positions), 0, topmost)
    scores = jnp.where(corner, ar_pos, jnp.where(vacant, (topmost + 2) * positions + ar_pos, (noise + 1) * positions + ar_pos))
    ranks = jnp.argsort(jnp.argsort(scores, axis=-1), axis=-1)
    occupied = ranks < NB
    local = jnp.cumsum(occupied.astype(jnp.int32), axis=-1) - 1
    local = jnp.where(occupied, local, NB).astype(jnp.int32)
    slots = jnp.argsort(jnp.where(occupied, ar_pos, ar_pos + positions), axis=-1)[..., :NB].astype(jnp.int32)
    local = local.reshape(N_SLAB, N_COL, BX, BY, BZ)
    fcol = BX * BZ
    fslab = (BY + 2) * BZ
    grid_xz = jnp.arange(BX, dtype=jnp.int32)[:, None] * BZ + jnp.arange(BZ, dtype=jnp.int32)[None, :]
    low_col = jnp.broadcast_to((NB + 1 + grid_xz)[None, None, :, None, :], (N_SLAB, N_COL, BX, 1, BZ))
    high_col = low_col + fcol
    widened = jnp.concatenate([low_col, local, high_col], axis=3)
    grid_yz = jnp.arange(BY + 2, dtype=jnp.int32)[:, None] * BZ + jnp.arange(BZ, dtype=jnp.int32)[None, :]
    low_slab = jnp.broadcast_to((NB + 1 + 2 * fcol + grid_yz)[None, None, None, :, :], (N_SLAB, N_COL, 1, BY + 2, BZ))
    high_slab = low_slab + fslab
    full = jnp.concatenate([low_slab, widened, high_slab], axis=2)
    full = jnp.pad(full, ((0, 0), (0, 0), (0, 0), (0, 0), (1, 1)), constant_values=NB)
    full = full.reshape(N_SLAB, N_COL, -1)
    col_table = jnp.stack([local[:, :, :, 0, :], local[:, :, :, BY - 1, :]], axis=2).reshape(N_SLAB, N_COL, 2, fcol)
    slab_table = jnp.stack([widened[:, :, 0], widened[:, :, BX - 1]], axis=2).reshape(N_SLAB, N_COL, 2, fslab)
    slot_x = slots // (BY * BZ)
    slot_y = slots // BZ % BY
    slot_z = slots % BZ
    tables = []
    for offset in range(27):
        step_x = offset // 9 - 1
        step_y = offset // 3 % 3 - 1
        step_z = offset % 3 - 1
        flat = ((slot_x + step_x + 1) * (BY + 2) + slot_y + step_y + 1) * (BZ + 2) + slot_z + step_z + 1
        tables.append(jnp.take_along_axis(full, flat, axis=-1))
    neighbour_table = jnp.stack(tables, axis=2)
    cell_table = slot_x // 4 * (CY * CZ) + slot_y // 4 * CZ + slot_z // 4
    return (neighbour_table, col_table, slab_table, cell_table)


def to_layout(array):
    return array.transpose(2, 0, 1, 3).reshape(array.shape[2], -1).astype(jnp.int32)


def draw_neighbours(key, part):
    return to_layout(brick_geometry(key)[0])


def draw_col_send(key, part):
    return to_layout(brick_geometry(key)[1])


def draw_slab_send(key, part):
    return to_layout(brick_geometry(key)[2])


def draw_coarse_map(key, part):
    return brick_geometry(key)[3].reshape(-1).astype(jnp.int32)


def draw_coupling(key, part):
    shape = (LUMPED_BOXES, NCY, CZ)
    share = 0.5
    smooth_eigenvectors = jax.random.uniform(jax.random.fold_in(key, 31), (1, NCY, CZ), dtype=jnp.float32) < share
    spread = jnp.exp(jax.random.uniform(jax.random.fold_in(key, 32), shape, dtype=jnp.float32, minval=math.log(0.5), maxval=math.log(2.0)))
    gentle_shrink_factor = 1.0 - 1.5 * spread / LUMPED_BOXES
    sharp_shrink_factor = jax.random.uniform(jax.random.fold_in(key, 33), shape, dtype=jnp.float32, minval=0.2, maxval=0.6)
    flagged_places = jax.random.randint(jax.random.fold_in(key, 34), (3, 1, NCY, CZ), 0, LUMPED_BOXES)
    spike_span = jnp.any(jnp.arange(LUMPED_BOXES)[None, :, None, None] == flagged_places, axis=0)
    falloff_size = jax.random.uniform(jax.random.fold_in(key, 35), shape, dtype=jnp.float32, minval=0.5, maxval=0.8)
    return (jnp.where(smooth_eigenvectors, gentle_shrink_factor, sharp_shrink_factor) * jnp.where(spike_span, falloff_size, 1.0)).astype(jnp.float32)


def block_scale(own_key, shape, pieces, smallest, largest):
    factor_of = 1.0
    for axis_at, blocks in pieces:
        steps = jax.random.uniform(jax.random.fold_in(jax.random.fold_in(own_key, 6), axis_at), (blocks,), jnp.float32, smallest / len(pieces), largest / len(pieces))
        factor_of = factor_of * jnp.repeat(jnp.exp(steps), shape[axis_at] // blocks).reshape((-1,) + (1,) * (len(shape) - 1 - axis_at))
    return factor_of


def scatter_about(own_key, dims, scale, reach, shards=(), held_as=jnp.bfloat16):
    values = scale * jax.random.normal(own_key, dims, jnp.float32)
    if shards:
        values = values * block_scale(own_key, dims, shards, -0.22, 0.18)
    return jnp.clip(values, -reach, reach).astype(held_as)


def setup_inputs(seed: int = 0) -> dict:
    arg_keys = jax.random.split(jax.random.key(seed), 10)
    rhs = scatter_about(arg_keys[0], (64, NB * N_SLAB * N_COL), 1.0, 6.0, ((1, 512),), jnp.float32)
    start = scatter_about(arg_keys[1], (64, NB * N_SLAB * N_COL), 0.5, 4.0, ((1, 512),), jnp.float32)
    screen = jnp.clip(jnp.exp(math.log(5.0) - 3.218876 * jax.random.uniform(arg_keys[2], (64, NB * N_SLAB * N_COL), jnp.float32) ** block_scale(arg_keys[2], (64, NB * N_SLAB * N_COL), ((1, 512),), -0.2, 0.2)), 0.2, 5.0)
    neighbours = draw_neighbours(jax.random.fold_in(arg_keys[9], 71), 0)
    col_send = draw_col_send(jax.random.fold_in(arg_keys[9], 71), 0)
    slab_send = draw_slab_send(jax.random.fold_in(arg_keys[9], 71), 0)
    coarse_map = draw_coarse_map(jax.random.fold_in(arg_keys[9], 71), 0)
    coupling = draw_coupling(jax.random.fold_in(arg_keys[9], 71), 0)
    coarse_scale = jnp.clip(jnp.exp(math.log(0.2) - 1.3862944 * jax.random.uniform(arg_keys[8], (LUMPED_BOXES, NCY, CZ), jnp.float32) ** block_scale(arg_keys[8], (LUMPED_BOXES, NCY, CZ), ((0, 64), (1, 8)), -0.2, 0.2)), 0.05, 0.2)
    return dict(rhs=rhs, start=start, screen=screen, neighbours=neighbours, col_send=col_send, slab_send=slab_send, coarse_map=coarse_map, coupling=coupling, coarse_scale=coarse_scale)


relax_weight = 0.5

def stencil_table():
    masses = np.array([11.0 / 20.0, 13.0 / 60.0, 1.0 / 120.0])
    slopes = np.array([1.0, -1.0 / 3.0, -1.0 / 6.0])
    coeffs = np.arange(64)
    along_x = coeffs // 16
    along_y = coeffs // 4 % 4
    along_z = coeffs % 4
    offsets = np.arange(27)
    shift_x = offsets // 9 - 1
    shift_y = offsets // 3 % 3 - 1
    shift_z = offsets % 3 - 1
    dist_x = 4 * shift_x[None, :, None] + along_x[None, None, :] - along_x[:, None, None]
    dist_y = 4 * shift_y[None, :, None] + along_y[None, None, :] - along_y[:, None, None]
    dist_z = 4 * shift_z[None, :, None] + along_z[None, None, :] - along_z[:, None, None]
    inside = (np.abs(dist_x) <= 2) & (np.abs(dist_y) <= 2) & (np.abs(dist_z) <= 2)
    mass_x = masses[np.minimum(np.abs(dist_x), 2)]
    mass_y = masses[np.minimum(np.abs(dist_y), 2)]
    mass_z = masses[np.minimum(np.abs(dist_z), 2)]
    slope_x = slopes[np.minimum(np.abs(dist_x), 2)]
    slope_y = slopes[np.minimum(np.abs(dist_y), 2)]
    slope_z = slopes[np.minimum(np.abs(dist_z), 2)]
    values = slope_x * mass_y * mass_z + mass_x * slope_y * mass_z + mass_x * mass_y * slope_z
    return np.where(inside, values, 0.0).astype(np.float32)

def from_lower(stacked, strip_axis):
    zeros = jnp.zeros_like(lax.slice_in_dim(stacked, 0, 1, axis=strip_axis))
    return jnp.concatenate([zeros, lax.slice_in_dim(stacked, 0, stacked.shape[strip_axis] - 1, axis=strip_axis)], strip_axis)

def from_upper(stacked, strip_axis):
    zeros = jnp.zeros_like(lax.slice_in_dim(stacked, 0, 1, axis=strip_axis))
    return jnp.concatenate([lax.slice_in_dim(stacked, 1, stacked.shape[strip_axis], axis=strip_axis), zeros], strip_axis)

def reference(rhs, start, screen, neighbours, col_send, slab_send, coarse_map, coupling, coarse_scale):
    slabs = N_SLAB
    columns = N_COL

    def per_block(array, width):
        return array.reshape(array.shape[0], slabs, columns, width).transpose(1, 2, 0, 3)
    table_np = stencil_table()
    stencil = jnp.asarray(table_np)
    centre = float(table_np[0, 13, 0])
    rhs_blocks = per_block(rhs, NB)
    start_blocks = per_block(start, NB)
    screen_blocks = per_block(screen, NB)
    index_blocks = per_block(neighbours, NB).reshape(slabs * columns, 27, NB)
    col_blocks = per_block(col_send, FCOL)
    slab_blocks = per_block(slab_send, FSLAB)
    cell_blocks = coarse_map.reshape(slabs, columns, NB)
    diagonal = centre + screen_blocks
    take_cols = jax.vmap(jax.vmap(lambda source, index: jnp.take(source, index, axis=1)))

    def operate(field):
        zero_col = jnp.zeros((slabs, columns, 64, 1), jnp.float32)
        base_cols = jnp.concatenate([field, zero_col], -1)
        col_low = take_cols(base_cols, col_blocks[:, :, 0])
        col_high = take_cols(base_cols, col_blocks[:, :, 1])
        widened = jnp.concatenate([base_cols, from_lower(col_high, 1), from_upper(col_low, 1)], -1)
        slab_low = take_cols(widened, slab_blocks[:, :, 0])
        slab_high = take_cols(widened, slab_blocks[:, :, 1])
        extended = jnp.concatenate([widened, from_lower(slab_high, 0), from_upper(slab_low, 0)], -1)

        def local_apply(items):
            ext_one, index_one = items
            gathered = jnp.take(ext_one, index_one.reshape(-1), axis=1).reshape(64, 27, NB)
            return jnp.einsum('ioj,jon->in', stencil, gathered, precision=lax.Precision.HIGHEST)
        result = lax.map(local_apply, (extended.reshape(slabs * columns, 64, EXT), index_blocks))
        return result.reshape(slabs, columns, 64, NB) + screen_blocks * field
    field = start_blocks
    for sweep in range(SWEEPS):
        field = field + relax_weight * (rhs_blocks - operate(field)) / diagonal
    residual = rhs_blocks - operate(field)
    brick_mean = jnp.sum(residual, axis=2) / 64.0
    summed = jax.vmap(jax.vmap(lambda values, index: jax.ops.segment_sum(values, index, num_segments=CELLS)))(brick_mean, cell_blocks)
    coarse = summed.reshape(slabs, columns, CX, CY, CZ).transpose(0, 2, 1, 3, 4).reshape(LUMPED_BOXES, NCY, CZ)
    eye_rows = jnp.eye(NCY, dtype=jnp.float32)
    ymatrix = 2.5 * eye_rows - jnp.eye(NCY, k=1, dtype=jnp.float32) - jnp.eye(NCY, k=-1, dtype=jnp.float32)
    factor = jnp.linalg.cholesky(ymatrix)
    inverse = jax.scipy.linalg.cho_solve((factor, True), eye_rows)
    mixed = jnp.einsum('yk,xkz->xyz', inverse, coarse, precision=lax.Precision.HIGHEST)

    def forward(carry, items):
        value, weight = items
        carry = value + weight * carry
        return (carry, carry)

    def backward(carry, items):
        value, weight, pivot = items
        carry = pivot * value + weight * carry
        return (carry, carry)
    zero_line = jnp.zeros((NCY, CZ), jnp.float32)
    final_state, lines = lax.scan(forward, zero_line, (mixed, coupling))
    final_state, correction = lax.scan(backward, zero_line, (lines, coupling, coarse_scale), reverse=True)
    per_cell = correction.reshape(slabs, CX, columns, CY, CZ).transpose(0, 2, 1, 3, 4).reshape(slabs, columns, CELLS)
    per_brick = jnp.take_along_axis(per_cell, cell_blocks, axis=-1)
    solution = field + per_brick[:, :, None, :]
    return solution.transpose(2, 0, 1, 3).reshape(64, slabs * columns * NB)
```

```python
import functools

import jax
import jax.numpy as jnp
import numpy as np
from jax import lax
from jax.experimental import pallas as pl
from jax.experimental.pallas import tpu as pltpu
from jax.sharding import PartitionSpec as P

MESH = pl.DeviceIdType.MESH
F32 = jnp.float32
BF16 = jnp.bfloat16
I32 = jnp.int32
NB = 512
FCOL = 128
FSLAB = 160
RELAX = 0.5
COL0 = NB + 1
SLAB_LOW = COL0 + 2 * FCOL
SLAB_HIGH = SLAB_LOW + FSLAB
NOWHERE = -1000


def stencil_table():
    masses = np.array([11.0 / 20.0, 13.0 / 60.0, 1.0 / 120.0])
    slopes = np.array([1.0, -1.0 / 3.0, -1.0 / 6.0])
    coeffs = np.arange(64)
    along = (coeffs // 16, coeffs // 4 % 4, coeffs % 4)
    offsets = np.arange(27)
    shift = (offsets // 9 - 1, offsets // 3 % 3 - 1, offsets % 3 - 1)
    dist = [
        4 * shift[k][None, :, None] + along[k][None, None, :] - along[k][:, None, None]
        for k in range(3)
    ]
    inside = (np.abs(dist[0]) <= 2) & (np.abs(dist[1]) <= 2) & (np.abs(dist[2]) <= 2)
    m = [masses[np.minimum(np.abs(d), 2)] for d in dist]
    s = [slopes[np.minimum(np.abs(d), 2)] for d in dist]
    values = s[0] * m[1] * m[2] + m[0] * s[1] * m[2] + m[0] * m[1] * s[2]
    return np.where(inside, values, 0.0)


def split_np(x):
    x = np.asarray(x, np.float32)
    high = x.astype(jnp.bfloat16)
    return high, (x - high.astype(np.float32)).astype(jnp.bfloat16)


def tables(n_col):
    stencil = stencil_table()
    packed = np.zeros((64, 512))
    for blk in range(8):
        sx, sy, sz = blk // 4, blk // 2 % 2, blk % 2
        for j in range(64):
            a, b, e = j // 16, j // 4 % 4, j % 4
            dx = sx * (1 if a < 2 else -1)
            dy = sy * (1 if b < 2 else -1)
            dz = sz * (1 if e < 2 else -1)
            packed[:, blk * 64 + j] = stencil[:, 9 * (dx + 1) + 3 * (dy + 1) + dz + 1, j]
    stack = np.concatenate(split_np(packed), 0)
    sums = np.zeros((32, 64))
    for o in range(27):
        sums[o] = stencil[:, 26 - o, :].sum(0)
    sums_stack = np.concatenate(split_np(sums), 0)
    rows = 2 * n_col
    ymatrix = 2.5 * np.eye(rows) - np.eye(rows, k=1) - np.eye(rows, k=-1)
    inverse = np.linalg.inv(ymatrix)
    weights = np.zeros((n_col, n_col, 8, 128), np.float32)
    for own in range(n_col):
        for src in range(n_col):
            for dc in range(3):
                c = src + dc - 1
                if not 0 <= c < n_col:
                    continue
                for lane in range(128):
                    k = lane % 64
                    if k >= 48:
                        continue
                    y = k // 4 % 2
                    y_src = y if lane < 64 else 1 - y
                    weights[own, src, dc, lane] = inverse[2 * own + y, 2 * c + y_src]
    return stack, sums_stack, weights, float(np.float32(stencil[0, 13, 0]))


def split(x):
    high = x.astype(BF16)
    return high, (x - high.astype(F32)).astype(BF16)


def lanes(x, index):
    return jnp.take_along_axis(x, index, axis=1, mode="promise_in_bounds")


def own_sources(v, dx, dy):
    if dx == 1:
        span = range(v, v + 3)
    elif dx == -1:
        span = range(v - 2, v + 1)
    elif dy == 1:
        span = range(v, v + 2)
    elif dy == -1:
        span = range(v - 1, v + 1)
    else:
        span = range(v - 1, v + 2)
    return [w for w in span if 0 <= w < 4]


def kernel(
    n_slab, n_col, centre,
    rhs_hbm, start_hbm, screen_hbm, nbr_hbm, colsend_hbm, slabsend_hbm, cells_hbm, coupling_ref, scale_ref,
    stack_hbm, sums_hbm, weights_hbm,
    out_ref,
    rhs, screen, step, nbr, colsend, slabsend, cells, stack, sums, weights,
    gath, fc, fs, rc, rs_raw, diag, rs, info_s, info_c, in_s, in_c, in_d,
    codes, line_own, line_all, line_w, mix_all, mix_own, row_own, row_all,
    load_sem, send_sem, halo_sem, info_sem, line_sem, mix_sem, row_sem,
):
    s = lax.axis_index("slab")
    c = lax.axis_index("col")
    s_up, s_dn = lax.rem(s + 1, n_slab), lax.rem(s + n_slab - 1, n_slab)
    c_up, c_dn = lax.rem(c + 1, n_col), lax.rem(c + n_col - 1, n_col)

    loads = [
        pltpu.make_async_copy(a, b, load_sem.at[k])
        for k, (a, b) in enumerate([
            (start_hbm, gath.at[pl.ds(0, 64)]),
            (colsend_hbm, colsend),
            (slabsend_hbm, slabsend),
            (cells_hbm, cells),
            (nbr_hbm, nbr),
            (screen_hbm, screen),
            (rhs_hbm, rhs),
            (stack_hbm, stack),
            (sums_hbm, sums),
            (weights_hbm.at[c], weights),
        ])
    ]
    for load in loads:
        load.start()

    barrier = pltpu.get_barrier_semaphore()

    def hello(device):
        pl.semaphore_signal(barrier, inc=1, device_id=device, device_id_type=MESH)

    for device in ((s_up, c_up), (s_up, c_dn), (s_dn, c_up), (s_dn, c_dn)):
        hello(device)

    @pl.loop(1, n_col)
    def _(d):
        hello((s, lax.rem(c + d, n_col)))

    @pl.loop(1, n_slab)
    def _(d):
        hello((lax.rem(s + d, n_slab), c))

    sub = lax.broadcasted_iota(I32, (8, 128), 0)
    lane = lax.broadcasted_iota(I32, (8, 128), 1)
    e_low = lax.rem(sub, 4) < 2

    line_row = jnp.zeros((8, 128), F32)
    for k in range(16):
        line_row = jnp.where(lane == k, coupling_ref[k // 8, k // 4 % 2, k % 4], line_row)
        line_row = jnp.where(lane == 16 + k, scale_ref[k // 8, k // 4 % 2, k % 4], line_row)
    line_own[...] = line_row

    def row8(ref, r, v):
        return jnp.broadcast_to(ref[pl.ds(r, 1), pl.ds(128 * v, 128)], (8, 128))

    for load in loads[:4]:
        load.wait()

    col_index = [row8(colsend, k, 0) for k in range(2)]
    slab_index = [[row8(slabsend, k, v) for v in range(2)] for k in range(2)]

    def pick(index, source, spans, empty):
        low, high = index & 127, index >> 7
        got = jnp.full((8, 128), empty)
        for v in spans:
            got = jnp.where(high == v, lanes(source(v), low), got)
        return got

    def faces(k):
        for a in range(4):
            for bh in range(2):
                t = 2 * a + bh
                source = lambda v: gath[pl.ds(8 * t, 8), pl.ds(128 * v, 128)]
                fc[k, a, bh] = pick(col_index[0 if bh == 0 else 1], source, range(4), 0.0)
                for w in range(2):
                    side = 0 if a < 2 else 1
                    fs[k, a, bh, :, pl.ds(128 * w, 128)] = pick(
                        slab_index[side][w], source, (0,) if side == 0 else (3,), 0.0
                    )

    faces(0)
    cell_source = lambda v: row8(cells, 0, v)
    for k in range(2):
        info_c[k] = pick(col_index[k], cell_source, range(4), NOWHERE)
        for w in range(2):
            got = pick(slab_index[k][w], cell_source, range(4), NOWHERE)
            info_s[k, :, pl.ds(128 * w, 128)] = jnp.where(sub == 0, slab_index[k][w], got)

    pl.semaphore_wait(barrier, 4 + (n_col - 1) + (n_slab - 1))

    def send(src, dst, sent, recv, device):
        copy = pltpu.make_async_remote_copy(
            src_ref=src, dst_ref=dst, send_sem=sent, recv_sem=recv, device_id=device, device_id_type=MESH
        )
        copy.start()
        return copy

    low2, high2 = pl.ds(0, 2), pl.ds(2, 2)

    def send_faces(k):
        return [
            send(src, dst, send_sem.at[8 * k + m], halo_sem.at[8 * k + m], device)
            for m, (src, dst, device) in enumerate([
                (fs.at[k, low2], rs_raw.at[k, low2], (s_dn, c)),
                (fs.at[k, high2], rs_raw.at[k, high2], (s_up, c)),
                (fc.at[k, low2, 0], diag.at[k, low2, 0], (s_dn, c_dn)),
                (fc.at[k, low2, 1], diag.at[k, low2, 1], (s_dn, c_up)),
                (fc.at[k, high2, 0], diag.at[k, high2, 0], (s_up, c_dn)),
                (fc.at[k, high2, 1], diag.at[k, high2, 1], (s_up, c_up)),
                (fc.at[k, :, 0], rc.at[k, :, 0], (s, c_dn)),
                (fc.at[k, :, 1], rc.at[k, :, 1], (s, c_up)),
            ])
        ]

    def bytes_of(ref, sem):
        return pltpu.make_async_copy(ref, ref, sem)

    copies = [send_faces(0)]
    infos = [
        send(src, dst, send_sem.at[16 + m], info_sem.at[m], device)
        for m, (src, dst, device) in enumerate([
            (info_s.at[0], in_s.at[0], (s_dn, c)),
            (info_s.at[1], in_s.at[1], (s_up, c)),
            (info_c.at[0], in_c.at[0], (s, c_dn)),
            (info_c.at[1], in_c.at[1], (s, c_up)),
            (info_c.at[0], in_d.at[0, 0], (s_dn, c_dn)),
            (info_c.at[1], in_d.at[0, 1], (s_dn, c_up)),
            (info_c.at[0], in_d.at[1, 0], (s_up, c_dn)),
            (info_c.at[1], in_d.at[1, 1], (s_up, c_up)),
        ])
    ]
    line_all[pl.ds(s, 1)] = line_own[pl.ds(0, 1)].reshape(1, 1, 128)

    @pl.loop(1, n_slab)
    def _(d):
        send(line_own.at[pl.ds(0, 1)], line_all.at[s], send_sem.at[24], line_sem, (lax.rem(s + d, n_slab), c))

    for load in loads[4:]:
        load.wait()

    def wait_halo(k):
        for copy in copies[k]:
            copy.wait_recv()

    none = -99
    code_cl = jnp.where(c > 0, 0, none)
    code_ch = jnp.where(c < n_col - 1, 1, none)
    code_sl = [jnp.where(s > 0, w, none) for w in range(2)]
    code_sh = [jnp.where(s < n_slab - 1, w, none) for w in range(2)]

    def pattern(dx, dy, sz, v):
        o = 9 * (dx + 1) + 3 * (dy + 1) + 1
        if sz == 0:
            return row8(nbr, o, v)
        return jnp.where(e_low, row8(nbr, o + 1, v), row8(nbr, o - 1, v))

    def groups():
        for v in range(4):
            for blk in range(1, 8):
                sx, sy, sz = blk // 4, blk // 2 % 2, blk % 2
                for dx in ((1, -1) if sx else (0,)):
                    for dy in ((1, -1) if sy else (0,)):
                        halves = range(4) if dx == 0 else ((0, 1) if dx == 1 else (2, 3))
                        bhs = (0, 1) if dy == 0 else ((0,) if dy == 1 else (1,))
                        yield v, blk, dx, dy, sz, [2 * a + bh for a in halves for bh in bhs]

    def gather_own():
        for v, blk, dx, dy, sz, rows in groups():
            index = pattern(dx, dy, sz, v)
            low, high = index & 127, index >> 7
            spans = own_sources(v, dx, dy)
            masks = {w: high == w for w in spans}
            for t in rows:
                got = jnp.zeros((8, 128), F32)
                for w in spans:
                    got = jnp.where(masks[w], lanes(gath[pl.ds(8 * t, 8), pl.ds(128 * w, 128)], low), got)
                gath[pl.ds(64 * blk + 8 * t, 8), pl.ds(128 * v, 128)] = got

    def merge_rims(k):
        for a in range(4):
            side = 0 if a < 2 else 1
            for bh in range(2):
                for w in range(2):
                    at = jnp.broadcast_to(in_s[side, pl.ds(0, 1), pl.ds(128 * w, 128)], (8, 128)) - COL0
                    hit = (at >> 7) == (code_ch if bh == 0 else code_cl)
                    rs[pl.ds(16 * a + 8 * bh, 8), pl.ds(128 * w, 128)] = jnp.where(
                        hit, lanes(diag[k, a, bh], at & 127), rs_raw[k, a, bh, :, pl.ds(128 * w, 128)]
                    )

    def gather_rims(k):
        for v, blk, dx, dy, sz, rows in groups():
            along = (dx == 1 and v == 3) or (dx == -1 and v == 0)
            if dy == 0 and not along:
                continue
            index = pattern(dx, dy, sz, v)
            if dy:
                at_c = index - COL0
                low_c = at_c & 127
                hit_c = (at_c >> 7) == (code_ch if dy == 1 else code_cl)
            if along:
                at_s = index - (SLAB_HIGH if dx == 1 else SLAB_LOW)
                low_s = at_s & 127
                hits = [(at_s >> 7) == code for code in (code_sh if dx == 1 else code_sl)]
            for t in rows:
                where = (pl.ds(64 * blk + 8 * t, 8), pl.ds(128 * v, 128))
                got = gath[where]
                if dy:
                    got = jnp.where(hit_c, lanes(rc[k, t // 2, t % 2], low_c), got)
                if along:
                    for w in range(2):
                        got = jnp.where(hits[w], lanes(rs[pl.ds(8 * t, 8), pl.ds(128 * w, 128)], low_s), got)
                gath[where] = got

    def sweep():
        high, low = split(gath[...])
        both = jnp.dot(stack[...], high, preferred_element_type=F32)
        total = both[:64] + both[64:] + jnp.dot(stack[pl.ds(0, 64)], low, preferred_element_type=F32)
        field = gath[pl.ds(0, 64)]
        return field + step[...] * (rhs[...] - total - screen[...] * field)

    step[...] = RELAX / (centre + screen[...])
    gather_own()
    for copy in infos[:2]:
        copy.wait_recv()
    wait_halo(0)
    merge_rims(0)
    gather_rims(0)
    gath[pl.ds(0, 64)] = sweep()
    faces(1)
    copies.append(send_faces(1))
    gather_own()

    for copy in infos[2:]:
        copy.wait_recv()
    own_codes = [row8(cells, 0, v) + 64 for v in range(4)]
    col_codes = [in_c[1] + 48, in_c[0] + 80]
    slab_codes = []
    for side in (1, 0):
        base = 0 if side == 1 else 96
        parts = []
        for w in range(2):
            at = jnp.broadcast_to(in_s[side, pl.ds(0, 1), pl.ds(128 * w, 128)], (8, 128)) - COL0
            part = jnp.broadcast_to(in_s[side, pl.ds(1, 1), pl.ds(128 * w, 128)], (8, 128)) + base + 16
            part = jnp.where((at >> 7) == 0, lanes(in_d[side, 1], at & 127) + base, part)
            part = jnp.where((at >> 7) == 1, lanes(in_d[side, 0], at & 127) + base + 32, part)
            parts.append(part)
        slab_codes.append(parts)
    for r in range(4):
        for v in range(4):
            if r < 3:
                index = nbr[pl.ds(8 * r, 8), pl.ds(128 * v, 128)]
            else:
                index = jnp.full((8, 128), NB)
                for k in range(3):
                    index = jnp.where(sub == k, row8(nbr, 24 + k, v), index)
            low, high = index & 127, index >> 7
            code = jnp.full((8, 128), NOWHERE)
            for w in range(4):
                code = jnp.where(high == w, lanes(own_codes[w], low), code)
            at = index - COL0
            for m in range(2):
                code = jnp.where((at >> 7) == m, lanes(col_codes[m], at & 127), code)
            if (r < 2 and v == 0) or (r >= 2 and v == 3):
                at = index - (SLAB_LOW if r < 2 else SLAB_HIGH)
                for w in range(2):
                    code = jnp.where((at >> 7) == w, lanes(slab_codes[0 if r < 2 else 1][w], at & 127), code)
            codes[pl.ds(8 * r, 8), pl.ds(128 * v, 128)] = code

    bytes_of(line_all.at[pl.ds(0, n_slab - 1)], line_sem).wait()
    all_rows = line_all[...].reshape(n_slab, 128)
    big_lane = lax.broadcasted_iota(I32, (n_slab, 128), 1)
    big_row = lax.broadcasted_iota(I32, (n_slab, 128), 0)
    spot = big_lane & 7
    c0, c1, p0, p1 = [lanes(all_rows, spot + 8 * k) for k in range(4)]
    first = big_lane < 64
    after, here = big_row > s, big_row == s

    def rows_down(x, d, fill):
        return jnp.where(big_row >= d, pltpu.roll(x, d, 0), fill)

    def rows_up(x, d, fill):
        return jnp.where(big_row < n_slab - d, pltpu.roll(x, n_slab - d, 0), fill)

    run = jnp.where(after, c0 * c1, jnp.where(here, jnp.where(first, c0 * c1, c1), 1.0))
    d = 1
    while d < n_slab:
        run = run * rows_down(run, d, 1.0)
        d *= 2
    run = rows_down(run, 1, 1.0)
    w0 = jnp.where(after, run, jnp.where(here & first, 1.0, 0.0))
    w1 = jnp.where(after, run * c0, jnp.where(here, jnp.where(first, c0, 1.0), 0.0))
    u0, u1 = p0 * w0, p1 * w1
    c0_next = rows_up(c0, 1, 0.0)
    tail, factor = u0 + c1 * u1, c1 * c0_next
    d = 1
    while d < n_slab:
        tail = tail + factor * rows_up(tail, d, 0.0)
        factor = factor * rows_up(factor, d, 0.0)
        d *= 2
    second = u1 + c0_next * rows_up(tail, 1, 0.0)
    give = jnp.where((big_lane & 8) == 0, tail, second)
    part = (big_lane & 63) >> 4
    line_w[...] = jnp.where(
        part == 0, rows_down(give, 1, 0.0), jnp.where(part == 1, give, jnp.where(part == 2, rows_up(give, 1, 0.0), 0.0))
    )

    wait_halo(1)
    merge_rims(1)
    gather_rims(1)
    field = sweep()
    gath[pl.ds(0, 64)] = field

    high, low = split(field)
    both = jnp.dot(sums[...], high, preferred_element_type=F32)
    given = both[:32] + both[32:] + jnp.dot(sums[pl.ds(0, 32)], low, preferred_element_type=F32)
    local = jnp.sum(rhs[...] - screen[...] * field, axis=0, keepdims=True)
    row_at = lax.broadcasted_iota(I32, (32, 512), 0)
    given = (jnp.where(row_at == 13, jnp.broadcast_to(local, (32, 512)), 0.0) - given) * (1.0 / 64.0)

    def fold(parts):
        for bit in (4, 2, 1):
            keep = (sub & bit) == 0
            merged = []
            for k in range(bit):
                one, two = parts[k], parts[k + bit]
                stay, go = jnp.where(keep, one, two), jnp.where(keep, two, one)
                if bit == 4:
                    merged.append(stay + pltpu.roll(go, 4, 0))
                else:
                    merged.append(stay + jnp.where(keep, pltpu.roll(go, 8 - bit, 0), pltpu.roll(go, bit, 0)))
            parts = merged
        return parts[0]

    reach = {
        (0, 0): ((0, 1, 2, 3), range(4)),
        (0, -1): ((0, 1, 2), range(4)),
        (0, 1): ((0, 1, 2, 3), range(4)),
        (-1, 0): ((0, 1), (0,)),
        (-1, -1): ((0,), (0,)),
        (-1, 1): ((0, 1), (0,)),
        (1, 0): ((2, 3), (3,)),
        (1, -1): ((2,), (3,)),
        (1, 1): ((3,), (3,)),
    }
    nought = jnp.zeros((8, 128), F32)
    stacked = []
    for dc in (-1, 0, 1):
        plain, swapped = [], []
        for ds in (-1, 0, 1):
            rs_of, vs_of = reach[(ds, dc)]
            base = 48 * (ds + 1) + 16 * (dc + 1)
            for x in range(2):
                parts = []
                for k in range(8):
                    acc = nought
                    for r in rs_of:
                        for v in vs_of:
                            hit = codes[pl.ds(8 * r, 8), pl.ds(128 * v, 128)] == base + 8 * x + k
                            acc = acc + jnp.where(hit, given[8 * r : 8 * r + 8, 128 * v : 128 * v + 128], 0.0)
                    parts.append(acc)
                total = fold(parts)
                plain.append(total)
                swapped.append(pltpu.roll(total, 4, 0))
        stacked += plain + [nought, nought] + swapped + [nought, nought]
    high, low = split(jnp.concatenate(stacked, axis=0))
    ones = jnp.ones((16, 128), BF16)
    across = (((1,), (1,)), ((), ()))
    summed = lax.dot_general(ones, high, across, preferred_element_type=F32) + lax.dot_general(
        ones, low, across, preferred_element_type=F32
    )
    message = jnp.where(
        sub == 0, summed[:8, :128], jnp.where(sub == 1, summed[:8, 128:256], jnp.where(sub == 2, summed[:8, 256:], 0.0))
    )
    mix_own[...] = message
    mix_all[pl.ds(c, 1)] = message.reshape(1, 8, 128)

    @pl.loop(1, n_col)
    def _(d):
        send(mix_own, mix_all.at[c], send_sem.at[25], mix_sem, (s, lax.rem(c + d, n_col)))

    bytes_of(mix_all.at[pl.ds(0, n_col - 1)], mix_sem).wait()
    mixed = jnp.zeros((8, 128), F32)
    for k in range(n_col):
        mixed = mixed + weights[k] * mix_all[k]
    row = jnp.sum(mixed, axis=0, keepdims=True)
    row = row + pltpu.roll(row, 64, 1)
    row_own[...] = row
    row_all[pl.ds(s, 1)] = row.reshape(1, 1, 128)

    @pl.loop(1, n_slab)
    def _(d):
        send(row_own, row_all.at[s], send_sem.at[26], row_sem, (lax.rem(s + d, n_slab), c))

    bytes_of(row_all.at[pl.ds(0, n_slab - 1)], row_sem).wait()
    corr = jnp.sum(line_w[...] * row_all[...].reshape(n_slab, 128), axis=0, keepdims=True)
    corr = corr + pltpu.roll(corr, 128 - 8, 1)
    corr = corr + pltpu.roll(corr, 128 - 16, 1) + pltpu.roll(corr, 128 - 32, 1)
    corr = jnp.broadcast_to(corr, (8, 128))
    for v in range(4):
        cell = row8(cells, 0, v)
        lift = lanes(corr, (cell >> 3) * 64 + (cell & 7))
        for t in range(8):
            at = (pl.ds(8 * t, 8), pl.ds(128 * v, 128))
            out_ref[at] = gath[at] + lift

    for copy in copies[0] + copies[1] + infos:
        copy.wait_send()
    bytes_of(line_all.at[pl.ds(0, n_slab - 1)], send_sem.at[24]).wait()
    bytes_of(mix_all.at[pl.ds(0, n_col - 1)], send_sem.at[25]).wait()
    bytes_of(row_all.at[pl.ds(0, n_slab - 1)], send_sem.at[26]).wait()


def solution(mesh):
    n_slab, n_col = mesh.shape["slab"], mesh.shape["col"]
    stack, sums, weights, centre = tables(n_col)

    def shards(rhs, start, screen, neighbours, col_send, slab_send, coarse_map, coupling, coarse_scale):
        anywhere = pl.BlockSpec(memory_space=pl.ANY)
        scalars = pl.BlockSpec(memory_space=pltpu.SMEM)
        vmem = pltpu.VMEM
        dma = pltpu.SemaphoreType.DMA
        return pl.pallas_call(
            functools.partial(kernel, n_slab, n_col, centre),
            out_shape=jax.ShapeDtypeStruct((64, NB), F32),
            in_specs=[anywhere] * 7 + [scalars] * 2 + [anywhere] * 3,
            out_specs=pl.BlockSpec(memory_space=pltpu.VMEM),
            scratch_shapes=[
                vmem((64, NB), F32),
                vmem((64, NB), F32),
                vmem((64, NB), F32),
                vmem((27, NB), I32),
                vmem((2, FCOL), I32),
                vmem((2, 256), I32),
                vmem((1, NB), I32),
                vmem((128, 512), BF16),
                vmem((64, 64), BF16),
                vmem((n_col, 8, 128), F32),
                vmem((512, NB), F32),
                vmem((2, 4, 2, 8, 128), F32),
                vmem((2, 4, 2, 8, 256), F32),
                vmem((2, 4, 2, 8, 128), F32),
                vmem((2, 4, 2, 8, 256), F32),
                vmem((2, 4, 2, 8, 128), F32),
                vmem((64, 256), F32),
                vmem((2, 8, 256), I32),
                vmem((2, 8, 128), I32),
                vmem((2, 8, 256), I32),
                vmem((2, 8, 128), I32),
                vmem((2, 2, 8, 128), I32),
                vmem((32, NB), I32),
                vmem((8, 128), F32),
                vmem((n_slab, 1, 128), F32),
                vmem((n_slab, 128), F32),
                vmem((n_col, 8, 128), F32),
                vmem((8, 128), F32),
                vmem((1, 128), F32),
                vmem((n_slab, 1, 128), F32),
                dma((10,)),
                dma((27,)),
                dma((16,)),
                dma((8,)),
                dma,
                dma,
                dma,
            ],
            compiler_params=pltpu.CompilerParams(
                collective_id=0, has_side_effects=True, vmem_limit_bytes=32 * 1024 * 1024
            ),
            cost_estimate=pl.CostEstimate(flops=10**8, bytes_accessed=10**6, transcendentals=0),
        )(
            rhs, start, screen, neighbours, col_send, jnp.pad(slab_send, ((0, 0), (0, 256 - FSLAB))),
            coarse_map.reshape(1, NB), coupling, coarse_scale,
            jnp.asarray(stack), jnp.asarray(sums), jnp.asarray(weights),
        )

    block = P(None, ("slab", "col"))
    line = P("slab", "col", None)
    placed = (block,) * 6 + (P(("slab", "col")), line, line)
    return jax.shard_map(shards, mesh=mesh, in_specs=placed, out_specs=block, check_vma=False)
```

```python
import functools

import jax
import jax.numpy as jnp
import numpy as np
from jax import lax
from jax.experimental import pallas as pl
from jax.experimental.pallas import tpu as pltpu
from jax.sharding import PartitionSpec as P

MESH = pl.DeviceIdType.MESH
F32 = jnp.float32
BF16 = jnp.bfloat16
I32 = jnp.int32
NB = 512
FCOL = 128
FSLAB = 160
RELAX = 0.5
COL0 = NB + 1
SLAB_LOW = COL0 + 2 * FCOL
SLAB_HIGH = SLAB_LOW + FSLAB
NOWHERE = -1000


def stencil_table():
    masses = np.array([11.0 / 20.0, 13.0 / 60.0, 1.0 / 120.0])
    slopes = np.array([1.0, -1.0 / 3.0, -1.0 / 6.0])
    coeffs = np.arange(64)
    along = (coeffs // 16, coeffs // 4 % 4, coeffs % 4)
    offsets = np.arange(27)
    shift = (offsets // 9 - 1, offsets // 3 % 3 - 1, offsets % 3 - 1)
    dist = [
        4 * shift[k][None, :, None] + along[k][None, None, :] - along[k][:, None, None]
        for k in range(3)
    ]
    inside = (np.abs(dist[0]) <= 2) & (np.abs(dist[1]) <= 2) & (np.abs(dist[2]) <= 2)
    m = [masses[np.minimum(np.abs(d), 2)] for d in dist]
    s = [slopes[np.minimum(np.abs(d), 2)] for d in dist]
    values = s[0] * m[1] * m[2] + m[0] * s[1] * m[2] + m[0] * m[1] * s[2]
    return np.where(inside, values, 0.0)


def split_np(x):
    x = np.asarray(x, np.float32)
    high = x.astype(jnp.bfloat16)
    return high, (x - high.astype(np.float32)).astype(jnp.bfloat16)


def tables(n_col):
    stencil = stencil_table()
    packed = np.zeros((64, 512))
    for blk in range(8):
        sx, sy, sz = blk // 4, blk // 2 % 2, blk % 2
        for j in range(64):
            a, b, e = j // 16, j // 4 % 4, j % 4
            dx = sx * (1 if a < 2 else -1)
            dy = sy * (1 if b < 2 else -1)
            dz = sz * (1 if e < 2 else -1)
            packed[:, blk * 64 + j] = stencil[:, 9 * (dx + 1) + 3 * (dy + 1) + dz + 1, j]
    stack = np.concatenate(split_np(packed), 0)
    sums = np.zeros((32, 64))
    for o in range(27):
        sums[o] = stencil[:, 26 - o, :].sum(0)
    sums_stack = np.concatenate(split_np(sums), 0)
    rows = 2 * n_col
    ymatrix = 2.5 * np.eye(rows) - np.eye(rows, k=1) - np.eye(rows, k=-1)
    inverse = np.linalg.inv(ymatrix)
    weights = np.zeros((n_col, n_col, 8, 128), np.float32)
    for own in range(n_col):
        for src in range(n_col):
            for dc in range(3):
                c = src + dc - 1
                if not 0 <= c < n_col:
                    continue
                for lane in range(128):
                    k = lane % 64
                    if k >= 48:
                        continue
                    y = k // 4 % 2
                    y_src = y if lane < 64 else 1 - y
                    weights[own, src, dc, lane] = inverse[2 * own + y, 2 * c + y_src]
    return stack, sums_stack, weights, float(np.float32(stencil[0, 13, 0]))


def split(x):
    high = x.astype(BF16)
    return high, (x - high.astype(F32)).astype(BF16)


def lanes(x, index):
    return jnp.take_along_axis(x, index, axis=1, mode="promise_in_bounds")


def own_sources(v, dx, dy):
    if dx == 1:
        span = range(v, v + 3)
    elif dx == -1:
        span = range(v - 2, v + 1)
    elif dy == 1:
        span = range(v, v + 2)
    elif dy == -1:
        span = range(v - 1, v + 1)
    else:
        span = range(v - 1, v + 2)
    return [w for w in span if 0 <= w < 4]


def kernel(
    n_slab, n_col, centre,
    rhs_hbm, start_hbm, screen_hbm, nbr_hbm, colsend_hbm, slabsend_hbm, cells_hbm, coupling_hbm, scale_hbm,
    stack_hbm, sums_hbm, weights_hbm,
    out_ref,
    rhs, screen, step, nbr, colsend, slabsend, cells, coupling_ref, scale_ref, stack, sums, weights,
    gath, fc, fs, rc, rs_raw, diag, rs, info_s, info_c, in_s, in_c, in_d,
    codes, line_own, line_all, line_w, mix_all, mix_own, row_own, row_all,
    load_sem, send_sem, halo_sem, info_sem, line_sem, mix_sem, row_sem,
):
    s = lax.axis_index("slab")
    c = lax.axis_index("col")
    s_up, s_dn = lax.rem(s + 1, n_slab), lax.rem(s + n_slab - 1, n_slab)
    c_up, c_dn = lax.rem(c + 1, n_col), lax.rem(c + n_col - 1, n_col)

    loads = [
        pltpu.make_async_copy(a, b, load_sem.at[k])
        for k, (a, b) in enumerate([
            (start_hbm, gath.at[pl.ds(0, 64)]),
            (colsend_hbm, colsend),
            (slabsend_hbm, slabsend),
            (cells_hbm, cells),
            (coupling_hbm, coupling_ref),
            (scale_hbm, scale_ref),
            (nbr_hbm, nbr),
            (screen_hbm, screen),
            (rhs_hbm, rhs),
            (stack_hbm, stack),
            (sums_hbm, sums),
            (weights_hbm.at[c], weights),
        ])
    ]
    for load in loads:
        load.start()

    barrier = pltpu.get_barrier_semaphore()

    def hello(device):
        pl.semaphore_signal(barrier, inc=1, device_id=device, device_id_type=MESH)

    for device in ((s_up, c_up), (s_up, c_dn), (s_dn, c_up), (s_dn, c_dn)):
        hello(device)

    @pl.loop(1, n_col)
    def _(d):
        hello((s, lax.rem(c + d, n_col)))

    @pl.loop(1, n_slab)
    def _(d):
        hello((lax.rem(s + d, n_slab), c))

    sub = lax.broadcasted_iota(I32, (8, 128), 0)
    lane = lax.broadcasted_iota(I32, (8, 128), 1)
    e_low = lax.rem(sub, 4) < 2

    def row8(ref, r, v):
        return jnp.broadcast_to(ref[pl.ds(r, 1), pl.ds(128 * v, 128)], (8, 128))

    for load in loads[:6]:
        load.wait()

    col_index = [row8(colsend, k, 0) for k in range(2)]
    beyond = jnp.full((1, 256 - FSLAB), NB)
    slab_index = [
        [
            row8(slabsend, k, 0),
            jnp.broadcast_to(jnp.concatenate([slabsend[pl.ds(k, 1), pl.ds(128, FSLAB - 128)], beyond], axis=1), (8, 128)),
        ]
        for k in range(2)
    ]

    line_row = jnp.zeros((8, 128), F32)
    for k in range(16):
        line_row = jnp.where(lane == k, coupling_ref[k // 8, k // 4 % 2, k % 4], line_row)
        line_row = jnp.where(lane == 16 + k, scale_ref[k // 8, k // 4 % 2, k % 4], line_row)
    line_own[...] = line_row

    def pick(index, source, spans, empty):
        low, high = index & 127, index >> 7
        got = jnp.full((8, 128), empty)
        for v in spans:
            got = jnp.where(high == v, lanes(source(v), low), got)
        return got

    def faces(k):
        for a in range(4):
            for bh in range(2):
                t = 2 * a + bh
                source = lambda v: gath[pl.ds(8 * t, 8), pl.ds(128 * v, 128)]
                fc[k, a, bh] = pick(col_index[0 if bh == 0 else 1], source, range(4), 0.0)
                for w in range(2):
                    side = 0 if a < 2 else 1
                    fs[k, a, bh, :, pl.ds(128 * w, 128)] = pick(
                        slab_index[side][w], source, (0,) if side == 0 else (3,), 0.0
                    )

    faces(0)
    cell_source = lambda v: row8(cells, 0, v)
    for k in range(2):
        info_c[k] = pick(col_index[k], cell_source, range(4), NOWHERE)
        for w in range(2):
            got = pick(slab_index[k][w], cell_source, range(4), NOWHERE)
            info_s[k, :, pl.ds(128 * w, 128)] = jnp.where(sub == 0, slab_index[k][w], got)

    pl.semaphore_wait(barrier, 4 + (n_col - 1) + (n_slab - 1))

    def send(src, dst, sent, recv, device):
        copy = pltpu.make_async_remote_copy(
            src_ref=src, dst_ref=dst, send_sem=sent, recv_sem=recv, device_id=device, device_id_type=MESH
        )
        copy.start()
        return copy

    low2, high2 = pl.ds(0, 2), pl.ds(2, 2)

    def send_faces(k):
        return [
            send(src, dst, send_sem.at[8 * k + m], halo_sem.at[8 * k + m], device)
            for m, (src, dst, device) in enumerate([
                (fs.at[k, low2], rs_raw.at[k, low2], (s_dn, c)),
                (fs.at[k, high2], rs_raw.at[k, high2], (s_up, c)),
                (fc.at[k, low2, 0], diag.at[k, low2, 0], (s_dn, c_dn)),
                (fc.at[k, low2, 1], diag.at[k, low2, 1], (s_dn, c_up)),
                (fc.at[k, high2, 0], diag.at[k, high2, 0], (s_up, c_dn)),
                (fc.at[k, high2, 1], diag.at[k, high2, 1], (s_up, c_up)),
                (fc.at[k, :, 0], rc.at[k, :, 0], (s, c_dn)),
                (fc.at[k, :, 1], rc.at[k, :, 1], (s, c_up)),
            ])
        ]

    def bytes_of(ref, sem):
        return pltpu.make_async_copy(ref, ref, sem)

    copies = [send_faces(0)]
    infos = [
        send(src, dst, send_sem.at[16 + m], info_sem.at[m], device)
        for m, (src, dst, device) in enumerate([
            (info_s.at[0], in_s.at[0], (s_dn, c)),
            (info_s.at[1], in_s.at[1], (s_up, c)),
            (info_c.at[0], in_c.at[0], (s, c_dn)),
            (info_c.at[1], in_c.at[1], (s, c_up)),
            (info_c.at[0], in_d.at[0, 0], (s_dn, c_dn)),
            (info_c.at[1], in_d.at[0, 1], (s_dn, c_up)),
            (info_c.at[0], in_d.at[1, 0], (s_up, c_dn)),
            (info_c.at[1], in_d.at[1, 1], (s_up, c_up)),
        ])
    ]
    line_all[pl.ds(s, 1)] = line_own[pl.ds(0, 1)].reshape(1, 1, 128)

    @pl.loop(1, n_slab)
    def _(d):
        send(line_own.at[pl.ds(0, 1)], line_all.at[s], send_sem.at[24], line_sem, (lax.rem(s + d, n_slab), c))

    for load in loads[6:]:
        load.wait()

    def wait_halo(k):
        for copy in copies[k]:
            copy.wait_recv()

    none = -99
    code_cl = jnp.where(c > 0, 0, none)
    code_ch = jnp.where(c < n_col - 1, 1, none)
    code_sl = [jnp.where(s > 0, w, none) for w in range(2)]
    code_sh = [jnp.where(s < n_slab - 1, w, none) for w in range(2)]

    def pattern(dx, dy, sz, v):
        o = 9 * (dx + 1) + 3 * (dy + 1) + 1
        if sz == 0:
            return row8(nbr, o, v)
        return jnp.where(e_low, row8(nbr, o + 1, v), row8(nbr, o - 1, v))

    def groups():
        for v in range(4):
            for blk in range(1, 8):
                sx, sy, sz = blk // 4, blk // 2 % 2, blk % 2
                for dx in ((1, -1) if sx else (0,)):
                    for dy in ((1, -1) if sy else (0,)):
                        halves = range(4) if dx == 0 else ((0, 1) if dx == 1 else (2, 3))
                        bhs = (0, 1) if dy == 0 else ((0,) if dy == 1 else (1,))
                        yield v, blk, dx, dy, sz, [2 * a + bh for a in halves for bh in bhs]

    def gather_own():
        for v, blk, dx, dy, sz, rows in groups():
            index = pattern(dx, dy, sz, v)
            low, high = index & 127, index >> 7
            spans = own_sources(v, dx, dy)
            masks = {w: high == w for w in spans}
            for t in rows:
                got = jnp.zeros((8, 128), F32)
                for w in spans:
                    got = jnp.where(masks[w], lanes(gath[pl.ds(8 * t, 8), pl.ds(128 * w, 128)], low), got)
                gath[pl.ds(64 * blk + 8 * t, 8), pl.ds(128 * v, 128)] = got

    def merge_rims(k):
        for a in range(4):
            side = 0 if a < 2 else 1
            for bh in range(2):
                for w in range(2):
                    at = jnp.broadcast_to(in_s[side, pl.ds(0, 1), pl.ds(128 * w, 128)], (8, 128)) - COL0
                    hit = (at >> 7) == (code_ch if bh == 0 else code_cl)
                    rs[pl.ds(16 * a + 8 * bh, 8), pl.ds(128 * w, 128)] = jnp.where(
                        hit, lanes(diag[k, a, bh], at & 127), rs_raw[k, a, bh, :, pl.ds(128 * w, 128)]
                    )

    def gather_rims(k):
        for v, blk, dx, dy, sz, rows in groups():
            along = (dx == 1 and v == 3) or (dx == -1 and v == 0)
            if dy == 0 and not along:
                continue
            index = pattern(dx, dy, sz, v)
            if dy:
                at_c = index - COL0
                low_c = at_c & 127
                hit_c = (at_c >> 7) == (code_ch if dy == 1 else code_cl)
            if along:
                at_s = index - (SLAB_HIGH if dx == 1 else SLAB_LOW)
                low_s = at_s & 127
                hits = [(at_s >> 7) == code for code in (code_sh if dx == 1 else code_sl)]
            for t in rows:
                where = (pl.ds(64 * blk + 8 * t, 8), pl.ds(128 * v, 128))
                got = gath[where]
                if dy:
                    got = jnp.where(hit_c, lanes(rc[k, t // 2, t % 2], low_c), got)
                if along:
                    for w in range(2):
                        got = jnp.where(hits[w], lanes(rs[pl.ds(8 * t, 8), pl.ds(128 * w, 128)], low_s), got)
                gath[where] = got

    def sweep():
        high, low = split(gath[...])
        both = jnp.dot(stack[...], high, preferred_element_type=F32)
        total = both[:64] + both[64:] + jnp.dot(stack[pl.ds(0, 64)], low, preferred_element_type=F32)
        field = gath[pl.ds(0, 64)]
        return field + step[...] * (rhs[...] - total - screen[...] * field)

    step[...] = RELAX / (centre + screen[...])
    gather_own()
    for copy in infos[:2]:
        copy.wait_recv()
    wait_halo(0)
    merge_rims(0)
    gather_rims(0)
    gath[pl.ds(0, 64)] = sweep()
    faces(1)
    copies.append(send_faces(1))
    gather_own()

    for copy in infos[2:]:
        copy.wait_recv()
    own_codes = [row8(cells, 0, v) + 64 for v in range(4)]
    col_codes = [in_c[1] + 48, in_c[0] + 80]
    slab_codes = []
    for side in (1, 0):
        base = 0 if side == 1 else 96
        parts = []
        for w in range(2):
            at = jnp.broadcast_to(in_s[side, pl.ds(0, 1), pl.ds(128 * w, 128)], (8, 128)) - COL0
            part = jnp.broadcast_to(in_s[side, pl.ds(1, 1), pl.ds(128 * w, 128)], (8, 128)) + base + 16
            part = jnp.where((at >> 7) == 0, lanes(in_d[side, 1], at & 127) + base, part)
            part = jnp.where((at >> 7) == 1, lanes(in_d[side, 0], at & 127) + base + 32, part)
            parts.append(part)
        slab_codes.append(parts)
    for r in range(4):
        for v in range(4):
            if r < 3:
                index = nbr[pl.ds(8 * r, 8), pl.ds(128 * v, 128)]
            else:
                index = jnp.full((8, 128), NB)
                for k in range(3):
                    index = jnp.where(sub == k, row8(nbr, 24 + k, v), index)
            low, high = index & 127, index >> 7
            code = jnp.full((8, 128), NOWHERE)
            for w in range(4):
                code = jnp.where(high == w, lanes(own_codes[w], low), code)
            at = index - COL0
            for m in range(2):
                code = jnp.where((at >> 7) == m, lanes(col_codes[m], at & 127), code)
            if (r < 2 and v == 0) or (r >= 2 and v == 3):
                at = index - (SLAB_LOW if r < 2 else SLAB_HIGH)
                for w in range(2):
                    code = jnp.where((at >> 7) == w, lanes(slab_codes[0 if r < 2 else 1][w], at & 127), code)
            codes[pl.ds(8 * r, 8), pl.ds(128 * v, 128)] = code

    bytes_of(line_all.at[pl.ds(0, n_slab - 1)], line_sem).wait()
    all_rows = line_all[...].reshape(n_slab, 128)
    big_lane = lax.broadcasted_iota(I32, (n_slab, 128), 1)
    big_row = lax.broadcasted_iota(I32, (n_slab, 128), 0)
    spot = big_lane & 7
    c0, c1, p0, p1 = [lanes(all_rows, spot + 8 * k) for k in range(4)]
    first = big_lane < 64
    after, here = big_row > s, big_row == s

    def rows_down(x, d, fill):
        return jnp.where(big_row >= d, pltpu.roll(x, d, 0), fill)

    def rows_up(x, d, fill):
        return jnp.where(big_row < n_slab - d, pltpu.roll(x, n_slab - d, 0), fill)

    run = jnp.where(after, c0 * c1, jnp.where(here, jnp.where(first, c0 * c1, c1), 1.0))
    d = 1
    while d < n_slab:
        run = run * rows_down(run, d, 1.0)
        d *= 2
    run = rows_down(run, 1, 1.0)
    w0 = jnp.where(after, run, jnp.where(here & first, 1.0, 0.0))
    w1 = jnp.where(after, run * c0, jnp.where(here, jnp.where(first, c0, 1.0), 0.0))
    u0, u1 = p0 * w0, p1 * w1
    c0_next = rows_up(c0, 1, 0.0)
    tail, factor = u0 + c1 * u1, c1 * c0_next
    d = 1
    while d < n_slab:
        tail = tail + factor * rows_up(tail, d, 0.0)
        factor = factor * rows_up(factor, d, 0.0)
        d *= 2
    second = u1 + c0_next * rows_up(tail, 1, 0.0)
    give = jnp.where((big_lane & 8) == 0, tail, second)
    part = (big_lane & 63) >> 4
    line_w[...] = jnp.where(
        part == 0, rows_down(give, 1, 0.0), jnp.where(part == 1, give, jnp.where(part == 2, rows_up(give, 1, 0.0), 0.0))
    )

    wait_halo(1)
    merge_rims(1)
    gather_rims(1)
    field = sweep()
    gath[pl.ds(0, 64)] = field

    high, low = split(field)
    both = jnp.dot(sums[...], high, preferred_element_type=F32)
    given = both[:32] + both[32:] + jnp.dot(sums[pl.ds(0, 32)], low, preferred_element_type=F32)
    local = jnp.sum(rhs[...] - screen[...] * field, axis=0, keepdims=True)
    row_at = lax.broadcasted_iota(I32, (32, 512), 0)
    given = (jnp.where(row_at == 13, jnp.broadcast_to(local, (32, 512)), 0.0) - given) * (1.0 / 64.0)

    def fold(parts):
        for bit in (4, 2, 1):
            keep = (sub & bit) == 0
            merged = []
            for k in range(bit):
                one, two = parts[k], parts[k + bit]
                stay, go = jnp.where(keep, one, two), jnp.where(keep, two, one)
                if bit == 4:
                    merged.append(stay + pltpu.roll(go, 4, 0))
                else:
                    merged.append(stay + jnp.where(keep, pltpu.roll(go, 8 - bit, 0), pltpu.roll(go, bit, 0)))
            parts = merged
        return parts[0]

    reach = {
        (0, 0): ((0, 1, 2, 3), range(4)),
        (0, -1): ((0, 1, 2), range(4)),
        (0, 1): ((0, 1, 2, 3), range(4)),
        (-1, 0): ((0, 1), (0,)),
        (-1, -1): ((0,), (0,)),
        (-1, 1): ((0, 1), (0,)),
        (1, 0): ((2, 3), (3,)),
        (1, -1): ((2,), (3,)),
        (1, 1): ((3,), (3,)),
    }
    nought = jnp.zeros((8, 128), F32)
    stacked = []
    for dc in (-1, 0, 1):
        plain, swapped = [], []
        for ds in (-1, 0, 1):
            rs_of, vs_of = reach[(ds, dc)]
            base = 48 * (ds + 1) + 16 * (dc + 1)
            for x in range(2):
                parts = []
                for k in range(8):
                    acc = nought
                    for r in rs_of:
                        for v in vs_of:
                            hit = codes[pl.ds(8 * r, 8), pl.ds(128 * v, 128)] == base + 8 * x + k
                            acc = acc + jnp.where(hit, given[8 * r : 8 * r + 8, 128 * v : 128 * v + 128], 0.0)
                    parts.append(acc)
                total = fold(parts)
                plain.append(total)
                swapped.append(pltpu.roll(total, 4, 0))
        stacked += plain + [nought, nought] + swapped + [nought, nought]
    high, low = split(jnp.concatenate(stacked, axis=0))
    ones = jnp.ones((16, 128), BF16)
    across = (((1,), (1,)), ((), ()))
    summed = lax.dot_general(ones, high, across, preferred_element_type=F32) + lax.dot_general(
        ones, low, across, preferred_element_type=F32
    )
    message = jnp.where(
        sub == 0, summed[:8, :128], jnp.where(sub == 1, summed[:8, 128:256], jnp.where(sub == 2, summed[:8, 256:], 0.0))
    )
    mix_own[...] = message
    mix_all[pl.ds(c, 1)] = message.reshape(1, 8, 128)

    @pl.loop(1, n_col)
    def _(d):
        send(mix_own, mix_all.at[c], send_sem.at[25], mix_sem, (s, lax.rem(c + d, n_col)))

    bytes_of(mix_all.at[pl.ds(0, n_col - 1)], mix_sem).wait()
    mixed = jnp.zeros((8, 128), F32)
    for k in range(n_col):
        mixed = mixed + weights[k] * mix_all[k]
    row = jnp.sum(mixed, axis=0, keepdims=True)
    row = row + pltpu.roll(row, 64, 1)
    row_own[...] = row
    row_all[pl.ds(s, 1)] = row.reshape(1, 1, 128)

    @pl.loop(1, n_slab)
    def _(d):
        send(row_own, row_all.at[s], send_sem.at[26], row_sem, (lax.rem(s + d, n_slab), c))

    bytes_of(row_all.at[pl.ds(0, n_slab - 1)], row_sem).wait()
    corr = jnp.sum(line_w[...] * row_all[...].reshape(n_slab, 128), axis=0, keepdims=True)
    corr = corr + pltpu.roll(corr, 128 - 8, 1)
    corr = corr + pltpu.roll(corr, 128 - 16, 1) + pltpu.roll(corr, 128 - 32, 1)
    corr = jnp.broadcast_to(corr, (8, 128))
    for v in range(4):
        cell = row8(cells, 0, v)
        lift = lanes(corr, (cell >> 3) * 64 + (cell & 7))
        for t in range(8):
            at = (pl.ds(8 * t, 8), pl.ds(128 * v, 128))
            out_ref[at] = gath[at] + lift

    for copy in copies[0] + copies[1] + infos:
        copy.wait_send()
    bytes_of(line_all.at[pl.ds(0, n_slab - 1)], send_sem.at[24]).wait()
    bytes_of(mix_all.at[pl.ds(0, n_col - 1)], send_sem.at[25]).wait()
    bytes_of(row_all.at[pl.ds(0, n_slab - 1)], send_sem.at[26]).wait()


def solution(mesh):
    n_slab, n_col = mesh.shape["slab"], mesh.shape["col"]
    stack, sums, weights, centre = tables(n_col)

    def shards(rhs, start, screen, neighbours, col_send, slab_send, coarse_map, coupling, coarse_scale):
        hbm = pl.BlockSpec(memory_space=pltpu.HBM)
        vmem = pltpu.VMEM
        dma = pltpu.SemaphoreType.DMA
        return pl.pallas_call(
            functools.partial(kernel, n_slab, n_col, centre),
            out_shape=jax.ShapeDtypeStruct((64, NB), F32),
            in_specs=[hbm] * 12,
            out_specs=pl.BlockSpec(memory_space=pltpu.VMEM),
            scratch_shapes=[
                vmem((64, NB), F32),
                vmem((64, NB), F32),
                vmem((64, NB), F32),
                vmem((27, NB), I32),
                vmem((2, FCOL), I32),
                vmem((2, FSLAB), I32),
                vmem((1, NB), I32),
                pltpu.SMEM((2, 2, 4), F32),
                pltpu.SMEM((2, 2, 4), F32),
                vmem((128, 512), BF16),
                vmem((64, 64), BF16),
                vmem((n_col, 8, 128), F32),
                vmem((512, NB), F32),
                vmem((2, 4, 2, 8, 128), F32),
                vmem((2, 4, 2, 8, 256), F32),
                vmem((2, 4, 2, 8, 128), F32),
                vmem((2, 4, 2, 8, 256), F32),
                vmem((2, 4, 2, 8, 128), F32),
                vmem((64, 256), F32),
                vmem((2, 8, 256), I32),
                vmem((2, 8, 128), I32),
                vmem((2, 8, 256), I32),
                vmem((2, 8, 128), I32),
                vmem((2, 2, 8, 128), I32),
                vmem((32, NB), I32),
                vmem((8, 128), F32),
                vmem((n_slab, 1, 128), F32),
                vmem((n_slab, 128), F32),
                vmem((n_col, 8, 128), F32),
                vmem((8, 128), F32),
                vmem((1, 128), F32),
                vmem((n_slab, 1, 128), F32),
                dma((12,)),
                dma((27,)),
                dma((16,)),
                dma((8,)),
                dma,
                dma,
                dma,
            ],
            compiler_params=pltpu.CompilerParams(
                collective_id=0, has_side_effects=True, vmem_limit_bytes=63 * 1024 * 1024
            ),
            cost_estimate=pl.CostEstimate(flops=10**8, bytes_accessed=10**6, transcendentals=0),
        )(
            rhs, start, screen, neighbours, col_send, slab_send,
            coarse_map.reshape(1, NB), coupling, coarse_scale,
            jnp.asarray(stack), jnp.asarray(sums), jnp.asarray(weights),
        )

    block = P(None, ("slab", "col"))
    line = P("slab", "col", None)
    placed = (block,) * 6 + (P(("slab", "col")), line, line)
    return jax.shard_map(shards, mesh=mesh, in_specs=placed, out_specs=block, check_vma=False)
```

```python
import functools

import jax
import jax.numpy as jnp
import numpy as np
from jax import lax
from jax.experimental import pallas as pl
from jax.experimental.pallas import tpu as pltpu
from jax.sharding import PartitionSpec as P

MESH = pl.DeviceIdType.MESH
F32 = jnp.float32
BF16 = jnp.bfloat16
I32 = jnp.int32
NB = 512
FCOL = 128
FSLAB = 160
RELAX = 0.5
COL0 = NB + 1
SLAB_LOW = COL0 + 2 * FCOL
SLAB_HIGH = SLAB_LOW + FSLAB
NOWHERE = -1000


def stencil_table():
    masses = np.array([11.0 / 20.0, 13.0 / 60.0, 1.0 / 120.0])
    slopes = np.array([1.0, -1.0 / 3.0, -1.0 / 6.0])
    coeffs = np.arange(64)
    along = (coeffs // 16, coeffs // 4 % 4, coeffs % 4)
    offsets = np.arange(27)
    shift = (offsets // 9 - 1, offsets // 3 % 3 - 1, offsets % 3 - 1)
    dist = [
        4 * shift[k][None, :, None] + along[k][None, None, :] - along[k][:, None, None]
        for k in range(3)
    ]
    inside = (np.abs(dist[0]) <= 2) & (np.abs(dist[1]) <= 2) & (np.abs(dist[2]) <= 2)
    m = [masses[np.minimum(np.abs(d), 2)] for d in dist]
    s = [slopes[np.minimum(np.abs(d), 2)] for d in dist]
    values = s[0] * m[1] * m[2] + m[0] * s[1] * m[2] + m[0] * m[1] * s[2]
    return np.where(inside, values, 0.0)


def split_np(x):
    x = np.asarray(x, np.float32)
    high = x.astype(jnp.bfloat16)
    return high, (x - high.astype(np.float32)).astype(jnp.bfloat16)


def tables(n_col):
    stencil = stencil_table()
    packed = np.zeros((64, 512))
    for blk in range(8):
        sx, sy, sz = blk // 4, blk // 2 % 2, blk % 2
        for j in range(64):
            a, b, e = j // 16, j // 4 % 4, j % 4
            dx = sx * (1 if a < 2 else -1)
            dy = sy * (1 if b < 2 else -1)
            dz = sz * (1 if e < 2 else -1)
            packed[:, blk * 64 + j] = stencil[:, 9 * (dx + 1) + 3 * (dy + 1) + dz + 1, j]
    stack = np.concatenate(split_np(packed), 0)
    sums = np.zeros((32, 64))
    for o in range(27):
        sums[o] = stencil[:, 26 - o, :].sum(0)
    sums_stack = np.concatenate(split_np(sums), 0)
    rows = 2 * n_col
    ymatrix = 2.5 * np.eye(rows) - np.eye(rows, k=1) - np.eye(rows, k=-1)
    inverse = np.linalg.inv(ymatrix)
    weights = np.zeros((n_col, n_col, 8, 128), np.float32)
    for own in range(n_col):
        for src in range(n_col):
            for dc in range(3):
                c = src + dc - 1
                if not 0 <= c < n_col:
                    continue
                for lane in range(128):
                    k = lane % 64
                    if k >= 48:
                        continue
                    y = k // 4 % 2
                    y_src = y if lane < 64 else 1 - y
                    weights[own, src, dc, lane] = inverse[2 * own + y, 2 * c + y_src]
    return stack, sums_stack, weights, float(np.float32(stencil[0, 13, 0]))


def split(x):
    high = x.astype(BF16)
    return high, (x - high.astype(F32)).astype(BF16)


def lanes(x, index):
    return jnp.take_along_axis(x, index, axis=1, mode="promise_in_bounds")


def own_sources(v, dx, dy):
    if dx == 1:
        span = range(v, v + 3)
    elif dx == -1:
        span = range(v - 2, v + 1)
    elif dy == 1:
        span = range(v, v + 2)
    elif dy == -1:
        span = range(v - 1, v + 1)
    else:
        span = range(v - 1, v + 2)
    return [w for w in span if 0 <= w < 4]


def kernel(
    n_slab, n_col, centre,
    rhs_hbm, start_hbm, screen_hbm, nbr_hbm, colsend_hbm, slabsend_hbm, cells_hbm, coupling_hbm, scale_hbm,
    stack_hbm, sums_hbm, weights_hbm,
    out_ref,
    rhs, screen, step, nbr, colsend, slabsend, cells, coupling_ref, scale_ref, stack, sums, weights,
    gath, fc, fs, rc, rs_raw, diag, rs, info_s, info_c, in_s, in_c, in_d,
    codes, line_own, line_all, line_w, mix_all, mix_own, row_own, row_all,
    load_sem, send_sem, halo_sem, info_sem, line_sem, mix_sem, row_sem, far_sem,
):
    s = lax.axis_index("slab")
    c = lax.axis_index("col")
    s_up, s_dn = lax.rem(s + 1, n_slab), lax.rem(s + n_slab - 1, n_slab)
    c_up, c_dn = lax.rem(c + 1, n_col), lax.rem(c + n_col - 1, n_col)

    loads = [
        pltpu.make_async_copy(a, b, load_sem.at[k])
        for k, (a, b) in enumerate([
            (start_hbm, gath.at[pl.ds(0, 64)]),
            (colsend_hbm, colsend),
            (slabsend_hbm, slabsend),
            (cells_hbm, cells),
            (coupling_hbm, coupling_ref),
            (scale_hbm, scale_ref),
            (nbr_hbm, nbr),
            (screen_hbm, screen),
            (rhs_hbm, rhs),
            (stack_hbm, stack),
            (sums_hbm, sums),
            (weights_hbm.at[c], weights),
        ])
    ]
    for load in loads:
        load.start()

    barrier = pltpu.get_barrier_semaphore()

    def hello(device):
        pl.semaphore_signal(barrier, inc=1, device_id=device, device_id_type=MESH)

    for device in ((s_up, c_up), (s_up, c_dn), (s_dn, c_up), (s_dn, c_dn)):
        hello(device)

    @pl.loop(1, n_col)
    def _(d):
        hello((s, lax.rem(c + d, n_col)))

    near = 8 if n_slab >= 32 else 1

    @pl.loop(1, near + 1)
    def _(d):
        hello((lax.rem(s + d, n_slab), c))
        hello((lax.rem(s + n_slab - d, n_slab), c))

    sub = lax.broadcasted_iota(I32, (8, 128), 0)
    lane = lax.broadcasted_iota(I32, (8, 128), 1)
    e_low = lax.rem(sub, 4) < 2

    def row8(ref, r, v):
        return jnp.broadcast_to(ref[pl.ds(r, 1), pl.ds(128 * v, 128)], (8, 128))

    for load in loads[:6]:
        load.wait()

    col_index = [row8(colsend, k, 0) for k in range(2)]
    beyond = jnp.full((1, 256 - FSLAB), NB)
    slab_index = [
        [
            row8(slabsend, k, 0),
            jnp.broadcast_to(jnp.concatenate([slabsend[pl.ds(k, 1), pl.ds(128, FSLAB - 128)], beyond], axis=1), (8, 128)),
        ]
        for k in range(2)
    ]

    line_row = jnp.zeros((8, 128), F32)
    for k in range(16):
        line_row = jnp.where(lane == k, coupling_ref[k // 8, k // 4 % 2, k % 4], line_row)
        line_row = jnp.where(lane == 16 + k, scale_ref[k // 8, k // 4 % 2, k % 4], line_row)
    line_own[...] = line_row

    def pick(index, source, spans, empty):
        low, high = index & 127, index >> 7
        got = jnp.full((8, 128), empty)
        for v in spans:
            got = jnp.where(high == v, lanes(source(v), low), got)
        return got

    def faces(k):
        for a in range(4):
            for bh in range(2):
                t = 2 * a + bh
                source = lambda v: gath[pl.ds(8 * t, 8), pl.ds(128 * v, 128)]
                fc[k, a, bh] = pick(col_index[0 if bh == 0 else 1], source, range(4), 0.0)
                for w in range(2):
                    side = 0 if a < 2 else 1
                    fs[k, a, bh, :, pl.ds(128 * w, 128)] = pick(
                        slab_index[side][w], source, (0,) if side == 0 else (3,), 0.0
                    )

    faces(0)
    cell_source = lambda v: row8(cells, 0, v)
    for k in range(2):
        info_c[k] = pick(col_index[k], cell_source, range(4), NOWHERE)
        for w in range(2):
            got = pick(slab_index[k][w], cell_source, range(4), NOWHERE)
            info_s[k, :, pl.ds(128 * w, 128)] = jnp.where(sub == 0, slab_index[k][w], got)

    pl.semaphore_wait(barrier, 4 + (n_col - 1) + 2 * near)

    reaches = []
    while near < n_slab // 2:
        reaches.append(near)
        near *= 2

    def tell(k):
        if k < len(reaches):
            for d in (reaches[k], n_slab - reaches[k]):
                pl.semaphore_signal(
                    far_sem.at[k], inc=1, device_id=(lax.rem(s + d, n_slab), c), device_id_type=MESH
                )

    def hear(k):
        if k < len(reaches):
            pl.semaphore_wait(far_sem.at[k], 2)

    tell(0)

    def send(src, dst, sent, recv, device):
        copy = pltpu.make_async_remote_copy(
            src_ref=src, dst_ref=dst, send_sem=sent, recv_sem=recv, device_id=device, device_id_type=MESH
        )
        copy.start()
        return copy

    low2, high2 = pl.ds(0, 2), pl.ds(2, 2)

    def send_faces(k):
        return [
            send(src, dst, send_sem.at[8 * k + m], halo_sem.at[8 * k + m], device)
            for m, (src, dst, device) in enumerate([
                (fs.at[k, low2], rs_raw.at[k, low2], (s_dn, c)),
                (fs.at[k, high2], rs_raw.at[k, high2], (s_up, c)),
                (fc.at[k, low2, 0], diag.at[k, low2, 0], (s_dn, c_dn)),
                (fc.at[k, low2, 1], diag.at[k, low2, 1], (s_dn, c_up)),
                (fc.at[k, high2, 0], diag.at[k, high2, 0], (s_up, c_dn)),
                (fc.at[k, high2, 1], diag.at[k, high2, 1], (s_up, c_up)),
                (fc.at[k, :, 0], rc.at[k, :, 0], (s, c_dn)),
                (fc.at[k, :, 1], rc.at[k, :, 1], (s, c_up)),
            ])
        ]

    def bytes_of(ref, sem):
        return pltpu.make_async_copy(ref, ref, sem)

    copies = [send_faces(0)]
    infos = [
        send(src, dst, send_sem.at[16 + m], info_sem.at[m], device)
        for m, (src, dst, device) in enumerate([
            (info_s.at[0], in_s.at[0], (s_dn, c)),
            (info_s.at[1], in_s.at[1], (s_up, c)),
            (info_c.at[0], in_c.at[0], (s, c_dn)),
            (info_c.at[1], in_c.at[1], (s, c_up)),
            (info_c.at[0], in_d.at[0, 0], (s_dn, c_dn)),
            (info_c.at[1], in_d.at[0, 1], (s_dn, c_up)),
            (info_c.at[0], in_d.at[1, 0], (s_up, c_dn)),
            (info_c.at[1], in_d.at[1, 1], (s_up, c_up)),
        ])
    ]
    for load in loads[6:]:
        load.wait()

    def wait_halo(k):
        for copy in copies[k]:
            copy.wait_recv()

    none = -99
    code_cl = jnp.where(c > 0, 0, none)
    code_ch = jnp.where(c < n_col - 1, 1, none)
    code_sl = [jnp.where(s > 0, w, none) for w in range(2)]
    code_sh = [jnp.where(s < n_slab - 1, w, none) for w in range(2)]

    def pattern(dx, dy, sz, v):
        o = 9 * (dx + 1) + 3 * (dy + 1) + 1
        if sz == 0:
            return row8(nbr, o, v)
        return jnp.where(e_low, row8(nbr, o + 1, v), row8(nbr, o - 1, v))

    def groups():
        for v in range(4):
            for blk in range(1, 8):
                sx, sy, sz = blk // 4, blk // 2 % 2, blk % 2
                for dx in ((1, -1) if sx else (0,)):
                    for dy in ((1, -1) if sy else (0,)):
                        halves = range(4) if dx == 0 else ((0, 1) if dx == 1 else (2, 3))
                        bhs = (0, 1) if dy == 0 else ((0,) if dy == 1 else (1,))
                        yield v, blk, dx, dy, sz, [2 * a + bh for a in halves for bh in bhs]

    def gather_own():
        for v, blk, dx, dy, sz, rows in groups():
            index = pattern(dx, dy, sz, v)
            low, high = index & 127, index >> 7
            spans = own_sources(v, dx, dy)
            masks = {w: high == w for w in spans}
            for t in rows:
                got = jnp.zeros((8, 128), F32)
                for w in spans:
                    got = jnp.where(masks[w], lanes(gath[pl.ds(8 * t, 8), pl.ds(128 * w, 128)], low), got)
                gath[pl.ds(64 * blk + 8 * t, 8), pl.ds(128 * v, 128)] = got

    def merge_rims(k):
        for a in range(4):
            side = 0 if a < 2 else 1
            for bh in range(2):
                for w in range(2):
                    at = jnp.broadcast_to(in_s[side, pl.ds(0, 1), pl.ds(128 * w, 128)], (8, 128)) - COL0
                    hit = (at >> 7) == (code_ch if bh == 0 else code_cl)
                    rs[pl.ds(16 * a + 8 * bh, 8), pl.ds(128 * w, 128)] = jnp.where(
                        hit, lanes(diag[k, a, bh], at & 127), rs_raw[k, a, bh, :, pl.ds(128 * w, 128)]
                    )

    def gather_rims(k):
        for v, blk, dx, dy, sz, rows in groups():
            along = (dx == 1 and v == 3) or (dx == -1 and v == 0)
            if dy == 0 and not along:
                continue
            index = pattern(dx, dy, sz, v)
            if dy:
                at_c = index - COL0
                low_c = at_c & 127
                hit_c = (at_c >> 7) == (code_ch if dy == 1 else code_cl)
            if along:
                at_s = index - (SLAB_HIGH if dx == 1 else SLAB_LOW)
                low_s = at_s & 127
                hits = [(at_s >> 7) == code for code in (code_sh if dx == 1 else code_sl)]
            for t in rows:
                where = (pl.ds(64 * blk + 8 * t, 8), pl.ds(128 * v, 128))
                got = gath[where]
                if dy:
                    got = jnp.where(hit_c, lanes(rc[k, t // 2, t % 2], low_c), got)
                if along:
                    for w in range(2):
                        got = jnp.where(hits[w], lanes(rs[pl.ds(8 * t, 8), pl.ds(128 * w, 128)], low_s), got)
                gath[where] = got

    def sweep():
        high, low = split(gath[...])
        both = jnp.dot(stack[...], high, preferred_element_type=F32)
        total = both[:64] + both[64:] + jnp.dot(stack[pl.ds(0, 64)], low, preferred_element_type=F32)
        field = gath[pl.ds(0, 64)]
        return field + step[...] * (rhs[...] - total - screen[...] * field)

    step[...] = RELAX / (centre + screen[...])
    gather_own()
    for copy in infos[:2]:
        copy.wait_recv()
    wait_halo(0)
    hear(0)
    tell(1)
    merge_rims(0)
    gather_rims(0)
    gath[pl.ds(0, 64)] = sweep()
    faces(1)
    copies.append(send_faces(1))
    gather_own()

    for copy in infos[2:]:
        copy.wait_recv()
    own_codes = [row8(cells, 0, v) + 64 for v in range(4)]
    col_codes = [in_c[1] + 48, in_c[0] + 80]
    slab_codes = []
    for side in (1, 0):
        base = 0 if side == 1 else 96
        parts = []
        for w in range(2):
            at = jnp.broadcast_to(in_s[side, pl.ds(0, 1), pl.ds(128 * w, 128)], (8, 128)) - COL0
            part = jnp.broadcast_to(in_s[side, pl.ds(1, 1), pl.ds(128 * w, 128)], (8, 128)) + base + 16
            part = jnp.where((at >> 7) == 0, lanes(in_d[side, 1], at & 127) + base, part)
            part = jnp.where((at >> 7) == 1, lanes(in_d[side, 0], at & 127) + base + 32, part)
            parts.append(part)
        slab_codes.append(parts)
    for r in range(4):
        for v in range(4):
            if r < 3:
                index = nbr[pl.ds(8 * r, 8), pl.ds(128 * v, 128)]
            else:
                index = jnp.full((8, 128), NB)
                for k in range(3):
                    index = jnp.where(sub == k, row8(nbr, 24 + k, v), index)
            low, high = index & 127, index >> 7
            code = jnp.full((8, 128), NOWHERE)
            for w in range(4):
                code = jnp.where(high == w, lanes(own_codes[w], low), code)
            at = index - COL0
            for m in range(2):
                code = jnp.where((at >> 7) == m, lanes(col_codes[m], at & 127), code)
            if (r < 2 and v == 0) or (r >= 2 and v == 3):
                at = index - (SLAB_LOW if r < 2 else SLAB_HIGH)
                for w in range(2):
                    code = jnp.where((at >> 7) == w, lanes(slab_codes[0 if r < 2 else 1][w], at & 127), code)
            codes[pl.ds(8 * r, 8), pl.ds(128 * v, 128)] = code

    wait_halo(1)
    hear(1)
    merge_rims(1)
    gather_rims(1)
    field = sweep()
    gath[pl.ds(0, 64)] = field

    high, low = split(field)
    both = jnp.dot(sums[...], high, preferred_element_type=F32)
    given = both[:32] + both[32:] + jnp.dot(sums[pl.ds(0, 32)], low, preferred_element_type=F32)
    local = jnp.sum(rhs[...] - screen[...] * field, axis=0, keepdims=True)
    row_at = lax.broadcasted_iota(I32, (32, 512), 0)
    given = (jnp.where(row_at == 13, jnp.broadcast_to(local, (32, 512)), 0.0) - given) * (1.0 / 64.0)

    def fold(parts):
        for bit in (4, 2, 1):
            keep = (sub & bit) == 0
            merged = []
            for k in range(bit):
                one, two = parts[k], parts[k + bit]
                stay, go = jnp.where(keep, one, two), jnp.where(keep, two, one)
                if bit == 4:
                    merged.append(stay + pltpu.roll(go, 4, 0))
                else:
                    merged.append(stay + jnp.where(keep, pltpu.roll(go, 8 - bit, 0), pltpu.roll(go, bit, 0)))
            parts = merged
        return parts[0]

    reach = {
        (0, 0): ((0, 1, 2, 3), range(4)),
        (0, -1): ((0, 1, 2), range(4)),
        (0, 1): ((0, 1, 2, 3), range(4)),
        (-1, 0): ((0, 1), (0,)),
        (-1, -1): ((0,), (0,)),
        (-1, 1): ((0, 1), (0,)),
        (1, 0): ((2, 3), (3,)),
        (1, -1): ((2,), (3,)),
        (1, 1): ((3,), (3,)),
    }
    nought = jnp.zeros((8, 128), F32)
    stacked = []
    for dc in (-1, 0, 1):
        plain, swapped = [], []
        for ds in (-1, 0, 1):
            rs_of, vs_of = reach[(ds, dc)]
            base = 48 * (ds + 1) + 16 * (dc + 1)
            for x in range(2):
                parts = []
                for k in range(8):
                    acc = nought
                    for r in rs_of:
                        for v in vs_of:
                            hit = codes[pl.ds(8 * r, 8), pl.ds(128 * v, 128)] == base + 8 * x + k
                            acc = acc + jnp.where(hit, given[8 * r : 8 * r + 8, 128 * v : 128 * v + 128], 0.0)
                    parts.append(acc)
                total = fold(parts)
                plain.append(total)
                swapped.append(pltpu.roll(total, 4, 0))
        stacked += plain + [nought, nought] + swapped + [nought, nought]
    high, low = split(jnp.concatenate(stacked, axis=0))
    ones = jnp.ones((16, 128), BF16)
    across = (((1,), (1,)), ((), ()))
    summed = lax.dot_general(ones, high, across, preferred_element_type=F32) + lax.dot_general(
        ones, low, across, preferred_element_type=F32
    )
    message = jnp.where(
        sub == 0, summed[:8, :128], jnp.where(sub == 1, summed[:8, 128:256], jnp.where(sub == 2, summed[:8, 256:], 0.0))
    )
    mix_own[...] = message
    mix_all[pl.ds(c, 1)] = message.reshape(1, 8, 128)

    @pl.loop(1, n_col)
    def _(d):
        send(mix_own, mix_all.at[c], send_sem.at[25], mix_sem, (s, lax.rem(c + d, n_col)))

    line_all[pl.ds(s, 1)] = line_own[pl.ds(0, 1)].reshape(1, 1, 128)

    @pl.loop(1, n_slab)
    def _(d):
        send(line_own.at[pl.ds(0, 1)], line_all.at[s], send_sem.at[24], line_sem, (lax.rem(s + d, n_slab), c))

    bytes_of(mix_all.at[pl.ds(0, n_col - 1)], mix_sem).wait()
    mixed = jnp.zeros((8, 128), F32)
    for k in range(n_col):
        mixed = mixed + weights[k] * mix_all[k]
    row = jnp.sum(mixed, axis=0, keepdims=True)
    row = row + pltpu.roll(row, 64, 1)
    row_own[...] = row
    row_all[pl.ds(s, 1)] = row.reshape(1, 1, 128)

    @pl.loop(1, n_slab)
    def _(d):
        send(row_own, row_all.at[s], send_sem.at[26], row_sem, (lax.rem(s + d, n_slab), c))

    bytes_of(line_all.at[pl.ds(0, n_slab - 1)], line_sem).wait()
    all_rows = line_all[...].reshape(n_slab, 128)
    big_lane = lax.broadcasted_iota(I32, (n_slab, 128), 1)
    big_row = lax.broadcasted_iota(I32, (n_slab, 128), 0)
    spot = big_lane & 7
    c0, c1, p0, p1 = [lanes(all_rows, spot + 8 * k) for k in range(4)]
    first = big_lane < 64
    after, here = big_row > s, big_row == s

    def rows_down(x, d, fill):
        return jnp.where(big_row >= d, pltpu.roll(x, d, 0), fill)

    def rows_up(x, d, fill):
        return jnp.where(big_row < n_slab - d, pltpu.roll(x, n_slab - d, 0), fill)

    run = jnp.where(after, c0 * c1, jnp.where(here, jnp.where(first, c0 * c1, c1), 1.0))
    d = 1
    while d < n_slab:
        run = run * rows_down(run, d, 1.0)
        d *= 2
    run = rows_down(run, 1, 1.0)
    w0 = jnp.where(after, run, jnp.where(here & first, 1.0, 0.0))
    w1 = jnp.where(after, run * c0, jnp.where(here, jnp.where(first, c0, 1.0), 0.0))
    u0, u1 = p0 * w0, p1 * w1
    c0_next = rows_up(c0, 1, 0.0)
    tail, factor = u0 + c1 * u1, c1 * c0_next
    d = 1
    while d < n_slab:
        tail = tail + factor * rows_up(tail, d, 0.0)
        factor = factor * rows_up(factor, d, 0.0)
        d *= 2
    second = u1 + c0_next * rows_up(tail, 1, 0.0)
    give = jnp.where((big_lane & 8) == 0, tail, second)
    part = (big_lane & 63) >> 4
    line_w[...] = jnp.where(
        part == 0, rows_down(give, 1, 0.0), jnp.where(part == 1, give, jnp.where(part == 2, rows_up(give, 1, 0.0), 0.0))
    )

    bytes_of(row_all.at[pl.ds(0, n_slab - 1)], row_sem).wait()
    corr = jnp.sum(line_w[...] * row_all[...].reshape(n_slab, 128), axis=0, keepdims=True)
    corr = corr + pltpu.roll(corr, 128 - 8, 1)
    corr = corr + pltpu.roll(corr, 128 - 16, 1) + pltpu.roll(corr, 128 - 32, 1)
    corr = jnp.broadcast_to(corr, (8, 128))
    for v in range(4):
        cell = row8(cells, 0, v)
        lift = lanes(corr, (cell >> 3) * 64 + (cell & 7))
        for t in range(8):
            at = (pl.ds(8 * t, 8), pl.ds(128 * v, 128))
            out_ref[at] = gath[at] + lift

    for copy in copies[0] + copies[1] + infos:
        copy.wait_send()
    bytes_of(line_all.at[pl.ds(0, n_slab - 1)], send_sem.at[24]).wait()
    bytes_of(mix_all.at[pl.ds(0, n_col - 1)], send_sem.at[25]).wait()
    bytes_of(row_all.at[pl.ds(0, n_slab - 1)], send_sem.at[26]).wait()


def solution(mesh):
    n_slab, n_col = mesh.shape["slab"], mesh.shape["col"]
    stack, sums, weights, centre = tables(n_col)

    def shards(rhs, start, screen, neighbours, col_send, slab_send, coarse_map, coupling, coarse_scale):
        hbm = pl.BlockSpec(memory_space=pltpu.HBM)
        vmem = pltpu.VMEM
        dma = pltpu.SemaphoreType.DMA
        return pl.pallas_call(
            functools.partial(kernel, n_slab, n_col, centre),
            out_shape=jax.ShapeDtypeStruct((64, NB), F32),
            in_specs=[hbm] * 12,
            out_specs=pl.BlockSpec(memory_space=pltpu.VMEM),
            scratch_shapes=[
                vmem((64, NB), F32),
                vmem((64, NB), F32),
                vmem((64, NB), F32),
                vmem((27, NB), I32),
                vmem((2, FCOL), I32),
                vmem((2, FSLAB), I32),
                vmem((1, NB), I32),
                pltpu.SMEM((2, 2, 4), F32),
                pltpu.SMEM((2, 2, 4), F32),
                vmem((128, 512), BF16),
                vmem((64, 64), BF16),
                vmem((n_col, 8, 128), F32),
                vmem((512, NB), F32),
                vmem((2, 4, 2, 8, 128), F32),
                vmem((2, 4, 2, 8, 256), F32),
                vmem((2, 4, 2, 8, 128), F32),
                vmem((2, 4, 2, 8, 256), F32),
                vmem((2, 4, 2, 8, 128), F32),
                vmem((64, 256), F32),
                vmem((2, 8, 256), I32),
                vmem((2, 8, 128), I32),
                vmem((2, 8, 256), I32),
                vmem((2, 8, 128), I32),
                vmem((2, 2, 8, 128), I32),
                vmem((32, NB), I32),
                vmem((8, 128), F32),
                vmem((n_slab, 1, 128), F32),
                vmem((n_slab, 128), F32),
                vmem((n_col, 8, 128), F32),
                vmem((8, 128), F32),
                vmem((1, 128), F32),
                vmem((n_slab, 1, 128), F32),
                dma((12,)),
                dma((27,)),
                dma((16,)),
                dma((8,)),
                dma,
                dma,
                dma,
                pltpu.SemaphoreType.REGULAR((2,)),
            ],
            compiler_params=pltpu.CompilerParams(
                collective_id=0, has_side_effects=True, vmem_limit_bytes=63 * 1024 * 1024
            ),
            cost_estimate=pl.CostEstimate(flops=10**8, bytes_accessed=10**6, transcendentals=0),
        )(
            rhs, start, screen, neighbours, col_send, slab_send,
            coarse_map.reshape(1, NB), coupling, coarse_scale,
            jnp.asarray(stack), jnp.asarray(sums), jnp.asarray(weights),
        )

    block = P(None, ("slab", "col"))
    line = P("slab", "col", None)
    placed = (block,) * 6 + (P(("slab", "col")), line, line)
    return jax.shard_map(shards, mesh=mesh, in_specs=placed, out_specs=block, check_vma=False)
```

```python
import functools

import jax
import jax.numpy as jnp
import numpy as np
from jax import lax
from jax.experimental import pallas as pl
from jax.experimental.pallas import tpu as pltpu
from jax.sharding import PartitionSpec as P

MESH = pl.DeviceIdType.MESH
F32 = jnp.float32
BF16 = jnp.bfloat16
I32 = jnp.int32
NB = 512
FCOL = 128
FSLAB = 160
RELAX = 0.5
COL0 = NB + 1
SLAB_LOW = COL0 + 2 * FCOL
SLAB_HIGH = SLAB_LOW + FSLAB
AT_CL, AT_CH, AT_SLAB, AT_DL, AT_DH, AT_NONE = 5, 6, 10, 11, 12, 13
BLOCKS = (0, 1, 4, 5, 2, 3, 6, 7)
NOWHERE = -1000


def stencil_table():
    masses = np.array([11.0 / 20.0, 13.0 / 60.0, 1.0 / 120.0])
    slopes = np.array([1.0, -1.0 / 3.0, -1.0 / 6.0])
    coeffs = np.arange(64)
    along = (coeffs // 16, coeffs // 4 % 4, coeffs % 4)
    offsets = np.arange(27)
    shift = (offsets // 9 - 1, offsets // 3 % 3 - 1, offsets % 3 - 1)
    dist = [
        4 * shift[k][None, :, None] + along[k][None, None, :] - along[k][:, None, None]
        for k in range(3)
    ]
    inside = (np.abs(dist[0]) <= 2) & (np.abs(dist[1]) <= 2) & (np.abs(dist[2]) <= 2)
    m = [masses[np.minimum(np.abs(d), 2)] for d in dist]
    s = [slopes[np.minimum(np.abs(d), 2)] for d in dist]
    values = s[0] * m[1] * m[2] + m[0] * s[1] * m[2] + m[0] * m[1] * s[2]
    return np.where(inside, values, 0.0)


def split_np(x):
    x = np.asarray(x, np.float32)
    high = x.astype(jnp.bfloat16)
    return high, (x - high.astype(np.float32)).astype(jnp.bfloat16)


def tables(n_col):
    stencil = stencil_table()
    packed = np.zeros((64, 512))
    for at, blk in enumerate(BLOCKS):
        sx, sy, sz = blk // 4, blk // 2 % 2, blk % 2
        for j in range(64):
            a, b, e = j // 16, j // 4 % 4, j % 4
            dx = sx * (1 if a < 2 else -1)
            dy = sy * (1 if b < 2 else -1)
            dz = sz * (1 if e < 2 else -1)
            packed[:, at * 64 + j] = stencil[:, 9 * (dx + 1) + 3 * (dy + 1) + dz + 1, j]
    stack = np.concatenate(split_np(packed), 0)
    sums = np.zeros((32, 64))
    for o in range(27):
        sums[o] = stencil[:, 26 - o, :].sum(0)
    sums_stack = np.concatenate(split_np(sums), 0)
    rows = 2 * n_col
    ymatrix = 2.5 * np.eye(rows) - np.eye(rows, k=1) - np.eye(rows, k=-1)
    inverse = np.linalg.inv(ymatrix)
    weights = np.zeros((n_col, n_col, 8, 128), np.float32)
    for own in range(n_col):
        for src in range(n_col):
            for dc in range(3):
                c = src + dc - 1
                if not 0 <= c < n_col:
                    continue
                for lane in range(128):
                    k = lane % 64
                    if k >= 48:
                        continue
                    y = k // 4 % 2
                    y_src = y if lane < 64 else 1 - y
                    weights[own, src, dc, lane] = inverse[2 * own + y, 2 * c + y_src]
    return stack, sums_stack, weights, float(np.float32(stencil[0, 13, 0]))


def split(x):
    high = x.astype(BF16)
    return high, (x - high.astype(F32)).astype(BF16)


def lanes(x, index):
    return jnp.take_along_axis(x, index, axis=1, mode="promise_in_bounds")


def own_sources(v, dx, dy):
    if dx == 1:
        span = range(v, v + 3)
    elif dx == -1:
        span = range(v - 2, v + 1)
    elif dy == 1:
        span = range(v, v + 2)
    elif dy == -1:
        span = range(v - 1, v + 1)
    else:
        span = range(v - 1, v + 2)
    return [w for w in span if 0 <= w < 4]


def kernel(
    n_slab, n_col, centre,
    rhs_hbm, start_hbm, screen_hbm, nbr_hbm, colsend_hbm, slabsend_hbm, cells_hbm, coupling_hbm, scale_hbm,
    stack_hbm, sums_hbm, weights_hbm,
    out_hbm,
    rhs, screen, step, nbr, colsend, slabsend, cells, coupling_ref, scale_ref, stack, sums, weights,
    gath, edge, base, nbn, fc, fs, rc, rs, diag, info_s, info_c, in_s, in_c, in_d,
    codes, line_own, line_all, line_w, mix_all, mix_own, row_own, row_all,
    load_sem, out_sem, send_sem, halo_sem, info_sem, line_sem, mix_sem, row_sem, far_sem,
):
    s = lax.axis_index("slab")
    c = lax.axis_index("col")
    s_up, s_dn = lax.rem(s + 1, n_slab), lax.rem(s + n_slab - 1, n_slab)
    c_up, c_dn = lax.rem(c + 1, n_col), lax.rem(c + n_col - 1, n_col)

    barrier = pltpu.get_barrier_semaphore()

    def hello(device):
        pl.semaphore_signal(barrier, inc=1, device_id=device, device_id_type=MESH)

    near = 4 if n_slab >= 32 else 1
    for device in ((s_up, c_up), (s_up, c_dn), (s_dn, c_up), (s_dn, c_dn)):
        hello(device)
    for d in range(1, near + 1):
        hello((lax.rem(s + d, n_slab), c))
        hello((lax.rem(s + n_slab - d, n_slab), c))
    hello((s, c_up))
    hello((s, c_dn))

    loads = [
        pltpu.make_async_copy(a, b, load_sem.at[k])
        for k, (a, b) in enumerate([
            (start_hbm, gath.at[pl.ds(0, 64)]),
            (colsend_hbm, colsend),
            (slabsend_hbm, slabsend),
            (cells_hbm, cells),
            (coupling_hbm, coupling_ref),
            (scale_hbm, scale_ref),
            (nbr_hbm, nbr),
            (screen_hbm, screen),
            (rhs_hbm, rhs),
            (stack_hbm, stack),
            (sums_hbm, sums),
            (weights_hbm.at[c], weights),
        ])
    ]
    for load in loads:
        load.start()

    sub = lax.broadcasted_iota(I32, (8, 128), 0)
    lane = lax.broadcasted_iota(I32, (8, 128), 1)
    e_low = lax.rem(sub, 4) < 2

    def row8(ref, r, v):
        return jnp.broadcast_to(ref[pl.ds(r, 1), pl.ds(128 * v, 128)], (8, 128))

    for load in loads[:6]:
        load.wait()

    col_index = [row8(colsend, k, 0) for k in range(2)]
    beyond = jnp.full((1, 256 - FSLAB), NB)
    slab_index = [
        [
            row8(slabsend, k, 0),
            jnp.broadcast_to(jnp.concatenate([slabsend[pl.ds(k, 1), pl.ds(128, FSLAB - 128)], beyond], axis=1), (8, 128)),
        ]
        for k in range(2)
    ]

    line_row = jnp.zeros((8, 128), F32)
    for k in range(16):
        line_row = jnp.where(lane == k, coupling_ref[k // 8, k // 4 % 2, k % 4], line_row)
        line_row = jnp.where(lane == 16 + k, scale_ref[k // 8, k // 4 % 2, k % 4], line_row)
    line_own[...] = line_row

    def pick(index, source, spans, empty):
        low, high = index & 127, index >> 7
        got = jnp.full((8, 128), empty)
        for v in spans:
            got = jnp.where(high == v, lanes(source(v), low), got)
        return got

    def faces(k):
        for a in range(4):
            for bh in range(2):
                t = 2 * a + bh
                source = lambda v: gath[pl.ds(8 * t, 8), pl.ds(128 * v, 128)]
                fs[k, a, bh] = source(0 if a < 2 else 3)
                fc[k, a, bh] = pick(col_index[0 if bh == 0 else 1], source, range(4), 0.0)

    faces(0)
    cell_source = lambda v: row8(cells, 0, v)
    for k in range(2):
        info_c[k] = pick(col_index[k], cell_source, range(4), NOWHERE)
        for w in range(2):
            info_s[k, :, pl.ds(128 * w, 128)] = jnp.where(sub == 0, slab_index[k][w], cell_source(3 * k))

    pl.semaphore_wait(barrier, 6 + 2 * near)

    reaches = []
    while near < n_slab // 2:
        reaches.append(near)
        near *= 2

    def tell(k):
        if k < len(reaches):
            for d in (reaches[k], n_slab - reaches[k]):
                pl.semaphore_signal(
                    far_sem.at[k], inc=1, device_id=(lax.rem(s + d, n_slab), c), device_id_type=MESH
                )

    def hear(k):
        if k < len(reaches):
            pl.semaphore_wait(far_sem.at[k], 2)

    across_far = n_col > 4

    tell(0)

    def send(src, dst, sent, recv, device):
        copy = pltpu.make_async_remote_copy(
            src_ref=src, dst_ref=dst, send_sem=sent, recv_sem=recv, device_id=device, device_id_type=MESH
        )
        copy.start()
        return copy

    low2, high2 = pl.ds(0, 2), pl.ds(2, 2)

    def send_faces(k):
        return [
            send(src, dst, send_sem.at[8 * k + m], halo_sem.at[8 * k + m], device)
            for m, (src, dst, device) in enumerate([
                (fc.at[k, low2, 0], diag.at[k, low2, 0], (s_dn, c_dn)),
                (fc.at[k, low2, 1], diag.at[k, low2, 1], (s_dn, c_up)),
                (fc.at[k, high2, 0], diag.at[k, high2, 0], (s_up, c_dn)),
                (fc.at[k, high2, 1], diag.at[k, high2, 1], (s_up, c_up)),
                (fs.at[k, low2], rs.at[k, low2], (s_dn, c)),
                (fs.at[k, high2], rs.at[k, high2], (s_up, c)),
                (fc.at[k, :, 0], rc.at[k, :, 0], (s, c_dn)),
                (fc.at[k, :, 1], rc.at[k, :, 1], (s, c_up)),
            ])
        ]

    def bytes_of(ref, sem):
        return pltpu.make_async_copy(ref, ref, sem)

    copies = [send_faces(0)]
    infos = [
        send(src, dst, send_sem.at[16 + m], info_sem.at[m], device)
        for m, (src, dst, device) in enumerate([
            (info_s.at[0], in_s.at[0], (s_dn, c)),
            (info_s.at[1], in_s.at[1], (s_up, c)),
            (info_c.at[0], in_c.at[0], (s, c_dn)),
            (info_c.at[1], in_c.at[1], (s, c_up)),
            (info_c.at[0], in_d.at[0, 0], (s_dn, c_dn)),
            (info_c.at[1], in_d.at[0, 1], (s_dn, c_up)),
            (info_c.at[0], in_d.at[1, 0], (s_up, c_dn)),
            (info_c.at[1], in_d.at[1, 1], (s_up, c_up)),
        ])
    ]
    for load in loads[6:]:
        load.wait()

    def wait_halo(k):
        for copy in copies[k]:
            copy.wait_recv()

    def place(there, at):
        return 128 * jnp.where(there, at, AT_NONE)

    above, below, right, left = s < n_slab - 1, s > 0, c < n_col - 1, c > 0

    def raw_rows(r, v):
        if r < 3:
            return nbr[pl.ds(8 * r, 8), pl.ds(128 * v, 128)]
        index = jnp.full((8, 128), NB)
        for k in range(3):
            index = jnp.where(sub == k, row8(nbr, 24 + k, v), index)
        return index

    def place_col(index):
        at = index - COL0
        got = jnp.where(index < NB, index, 128 * AT_NONE)
        got = jnp.where((at >> 7) == 0, place(left, AT_CL) + (at & 127), got)
        return jnp.where((at >> 7) == 1, place(right, AT_CH) + (at & 127), got)

    def place_slab(index, got, up):
        at = index - (SLAB_HIGH if up else SLAB_LOW)
        side, there = (0, above) if up else (1, below)
        listed = jnp.full((8, 128), NB)
        for w in range(2):
            table = jnp.broadcast_to(in_s[side, pl.ds(0, 1), pl.ds(128 * w, 128)], (8, 128))
            listed = jnp.where((at >> 7) == w, lanes(table, at & 127), listed)
        col = listed - COL0
        spot = jnp.where((listed >> 7) == (0 if up else 3), place(there, AT_SLAB) + (listed & 127), 128 * AT_NONE)
        spot = jnp.where((col >> 7) == 0, place(there & left, AT_DL) + (col & 127), spot)
        spot = jnp.where((col >> 7) == 1, place(there & right, AT_DH) + (col & 127), spot)
        return jnp.where((at >= 0) & (at < FSLAB), spot, got)

    def pattern(dx, dy, sz, v):
        o = 9 * (dx + 1) + 3 * (dy + 1) + 1
        if sz == 0:
            return row8(nbn, o, v)
        return jnp.where(e_low, row8(nbn, o + 1, v), row8(nbn, o - 1, v))

    def groups(v):
        for at, blk in enumerate(BLOCKS):
            if blk == 0:
                continue
            sx, sy, sz = blk // 4, blk // 2 % 2, blk % 2
            for dx in ((1, -1) if sx else (0,)):
                for dy in ((1, -1) if sy else (0,)):
                    halves = range(4) if dx == 0 else ((0, 1) if dx == 1 else (2, 3))
                    bhs = (0, 1) if dy == 0 else ((0,) if dy == 1 else (1,))
                    yield at, dx, dy, sz, [2 * a + bh for a in halves for bh in bhs]

    def gather_own():
        for v in range(4):
            for blk, dx, dy, sz, rows in groups(v):
                index = pattern(dx, dy, sz, v)
                low, high = index & 127, index >> 7
                spans = own_sources(v, dx, dy)
                masks = {w: high == w for w in spans}
                for t in rows:
                    got = jnp.zeros((8, 128), F32)
                    for w in spans:
                        got = jnp.where(masks[w], lanes(gath[pl.ds(8 * t, 8), pl.ds(128 * w, 128)], low), got)
                    gath[pl.ds(64 * blk + 8 * t, 8), pl.ds(128 * v, 128)] = got

    def gather_rims(k, v, slot, half):
        for blk, dx, dy, sz, rows in groups(v):
            along = (dx == 1 and v == 3) or (dx == -1 and v == 0)
            if dy == 0 and not along:
                continue
            index = pattern(dx, dy, sz, v)
            low, high = index & 127, index >> 7
            for t in rows:
                a, bh = t // 2, t % 2
                got = jnp.zeros((8, 128), F32)
                if dy:
                    got = jnp.where(high == (AT_CH if dy == 1 else AT_CL), lanes(rc[k, a, bh], low), got)
                if along:
                    got = jnp.where(high == AT_SLAB, lanes(rs[k, a, bh], low), got)
                    if dy:
                        got = jnp.where(high == (AT_DH if dy == 1 else AT_DL), lanes(diag[k, a, bh], low), got)
                edge[half, pl.ds(64 * (blk - 2) + 8 * t, 8), pl.ds(128 * slot, 128)] = got

    def product(source, rows):
        high, low = split(source)
        both = jnp.dot(stack[:, rows], high, preferred_element_type=F32)
        return both[:64] + both[64:] + jnp.dot(stack[pl.ds(0, 64), rows], low, preferred_element_type=F32)

    def sweep_own():
        gather_own()
        field = gath[pl.ds(0, 64)]
        total = product(gath[...], pl.ds(0, 512))
        base[...] = field + step[...] * (rhs[...] - total - screen[...] * field)

    def sweep_rims(k):
        for half, vs in ((0, (1, 2)), (1, (0, 3))):
            for slot, v in enumerate(vs):
                gather_rims(k, v, slot, half)
            first = 256 if half == 0 else 128
            total = product(edge[half, pl.ds(first - 128, 512 - first)], pl.ds(first, 512 - first))
            for slot, v in enumerate(vs):
                at = pl.ds(128 * v, 128)
                gath[pl.ds(0, 64), at] = base[:, at] - step[:, at] * total[:, 128 * slot : 128 * slot + 128]

    step[...] = RELAX / (centre + screen[...])
    edge[1, pl.ds(0, 128)] = jnp.zeros((128, 256), F32)
    for r in range(4):
        for v in range(4):
            nbn[pl.ds(8 * r, 8), pl.ds(128 * v, 128)] = place_col(raw_rows(r, v))
    sweep_own()
    for copy in infos[:2]:
        copy.wait_recv()
    for r in range(4):
        at = (pl.ds(8 * r, 8), pl.ds(0 if r < 2 else 384, 128))
        nbn[at] = place_slab(raw_rows(r, 0 if r < 2 else 3), nbn[at], r >= 2)
    wait_halo(0)
    hear(0)
    tell(1)
    if across_far:
        for d in (2, n_col - 2):
            pl.semaphore_signal(far_sem.at[3], inc=1, device_id=(s, lax.rem(c + d, n_col)), device_id_type=MESH)
    sweep_rims(0)
    faces(1)
    copies.append(send_faces(1))
    sweep_own()

    for copy in infos[2:]:
        copy.wait_recv()
    own_codes = [row8(cells, 0, v) + 64 for v in range(4)]
    col_codes = [in_c[1] + 48, in_c[0] + 80]
    for r in range(4):
        for v in range(4):
            index = nbn[pl.ds(8 * r, 8), pl.ds(128 * v, 128)]
            low, high = index & 127, index >> 7
            code = jnp.full((8, 128), NOWHERE)
            for w in range(4):
                code = jnp.where(high == w, lanes(own_codes[w], low), code)
            for w, at in enumerate((AT_CL, AT_CH)):
                code = jnp.where(high == at, lanes(col_codes[w], low), code)
            if (r < 2 and v == 0) or (r >= 2 and v == 3):
                side, first = (1, 0) if r < 2 else (0, 96)
                beside = jnp.broadcast_to(in_s[side, pl.ds(1, 1), pl.ds(0, 128)], (8, 128))
                code = jnp.where(high == AT_SLAB, lanes(beside, low) + first + 16, code)
                code = jnp.where(high == AT_DL, lanes(in_d[side, 1], low) + first, code)
                code = jnp.where(high == AT_DH, lanes(in_d[side, 0], low) + first + 32, code)
            codes[pl.ds(8 * r, 8), pl.ds(128 * v, 128)] = code

    hear(1)
    tell(2)
    wait_halo(1)
    sweep_rims(1)
    field = gath[pl.ds(0, 64)]

    high, low = split(field)
    both = jnp.dot(sums[...], high, preferred_element_type=F32)
    given = both[:32] + both[32:] + jnp.dot(sums[pl.ds(0, 32)], low, preferred_element_type=F32)
    local = jnp.sum(rhs[...] - screen[...] * field, axis=0, keepdims=True)
    row_at = lax.broadcasted_iota(I32, (32, 512), 0)
    given = (jnp.where(row_at == 13, jnp.broadcast_to(local, (32, 512)), 0.0) - given) * (1.0 / 64.0)

    def fold(parts):
        for bit in (4, 2, 1):
            keep = (sub & bit) == 0
            merged = []
            for k in range(bit):
                one, two = parts[k], parts[k + bit]
                stay, go = jnp.where(keep, one, two), jnp.where(keep, two, one)
                if bit == 4:
                    merged.append(stay + pltpu.roll(go, 4, 0))
                else:
                    merged.append(stay + jnp.where(keep, pltpu.roll(go, 8 - bit, 0), pltpu.roll(go, bit, 0)))
            parts = merged
        return parts[0]

    reach = {
        (0, 0): ((0, 1, 2, 3), range(4)),
        (0, -1): ((0, 1, 2), range(4)),
        (0, 1): ((0, 1, 2, 3), range(4)),
        (-1, 0): ((0, 1), (0,)),
        (-1, -1): ((0,), (0,)),
        (-1, 1): ((0, 1), (0,)),
        (1, 0): ((2, 3), (3,)),
        (1, -1): ((2,), (3,)),
        (1, 1): ((3,), (3,)),
    }
    nought = jnp.zeros((8, 128), F32)
    stacked = []
    for dc in (-1, 0, 1):
        plain, swapped = [], []
        for ds in (-1, 0, 1):
            rs_of, vs_of = reach[(ds, dc)]
            first_code = 48 * (ds + 1) + 16 * (dc + 1)
            for x in range(2):
                parts = []
                for k in range(8):
                    acc = nought
                    for r in rs_of:
                        for v in vs_of:
                            hit = codes[pl.ds(8 * r, 8), pl.ds(128 * v, 128)] == first_code + 8 * x + k
                            acc = acc + jnp.where(hit, given[8 * r : 8 * r + 8, 128 * v : 128 * v + 128], 0.0)
                    parts.append(acc)
                total = fold(parts)
                plain.append(total)
                swapped.append(pltpu.roll(total, 4, 0))
        stacked += plain + [nought, nought] + swapped + [nought, nought]
    high, low = split(jnp.concatenate(stacked, axis=0))
    ones = jnp.ones((16, 128), BF16)
    across = (((1,), (1,)), ((), ()))
    summed = lax.dot_general(ones, high, across, preferred_element_type=F32) + lax.dot_general(
        ones, low, across, preferred_element_type=F32
    )
    message = jnp.where(
        sub == 0, summed[:8, :128], jnp.where(sub == 1, summed[:8, 128:256], jnp.where(sub == 2, summed[:8, 256:], 0.0))
    )
    if across_far:
        pl.semaphore_wait(far_sem.at[3], 2)
    mix_own[...] = message
    mix_all[pl.ds(c, 1)] = message.reshape(1, 8, 128)

    @pl.loop(1, n_col)
    def _(d):
        send(mix_own, mix_all.at[c], send_sem.at[25], mix_sem, (s, lax.rem(c + d, n_col)))

    hear(2)
    line_all[pl.ds(s, 1)] = line_own[pl.ds(0, 1)].reshape(1, 1, 128)

    @pl.loop(1, n_slab)
    def _(d):
        send(line_own.at[pl.ds(0, 1)], line_all.at[s], send_sem.at[24], line_sem, (lax.rem(s + d, n_slab), c))

    bytes_of(mix_all.at[pl.ds(0, n_col - 1)], mix_sem).wait()
    mixed = jnp.zeros((8, 128), F32)
    for k in range(n_col):
        mixed = mixed + weights[k] * mix_all[k]
    row = jnp.sum(mixed, axis=0, keepdims=True)
    row = row + pltpu.roll(row, 64, 1)
    row_own[...] = row
    row_all[pl.ds(s, 1)] = row.reshape(1, 1, 128)

    @pl.loop(1, n_slab, unroll=9 if n_slab == 64 else 1)
    def _(d):
        send(row_own, row_all.at[s], send_sem.at[26], row_sem, (lax.rem(s + d, n_slab), c))

    bytes_of(line_all.at[pl.ds(0, n_slab - 1)], line_sem).wait()
    all_rows = line_all[...].reshape(n_slab, 128)
    big_lane = lax.broadcasted_iota(I32, (n_slab, 128), 1)
    big_row = lax.broadcasted_iota(I32, (n_slab, 128), 0)
    spot = big_lane & 7
    c0, c1, p0, p1 = [lanes(all_rows, spot + 8 * k) for k in range(4)]
    first = big_lane < 64
    after, here = big_row > s, big_row == s

    def rows_down(x, d, fill):
        return jnp.where(big_row >= d, pltpu.roll(x, d, 0), fill)

    def rows_up(x, d, fill):
        return jnp.where(big_row < n_slab - d, pltpu.roll(x, n_slab - d, 0), fill)

    run = jnp.where(after, c0 * c1, jnp.where(here, jnp.where(first, c0 * c1, c1), 1.0))
    d = 1
    while d < n_slab:
        run = run * rows_down(run, d, 1.0)
        d *= 2
    run = rows_down(run, 1, 1.0)
    w0 = jnp.where(after, run, jnp.where(here & first, 1.0, 0.0))
    w1 = jnp.where(after, run * c0, jnp.where(here, jnp.where(first, c0, 1.0), 0.0))
    u0, u1 = p0 * w0, p1 * w1
    c0_next = rows_up(c0, 1, 0.0)
    tail, factor = u0 + c1 * u1, c1 * c0_next
    d = 1
    while d < n_slab:
        tail = tail + factor * rows_up(tail, d, 0.0)
        factor = factor * rows_up(factor, d, 0.0)
        d *= 2
    second = u1 + c0_next * rows_up(tail, 1, 0.0)
    give = jnp.where((big_lane & 8) == 0, tail, second)
    part = (big_lane & 63) >> 4
    line_w[...] = jnp.where(
        part == 0, rows_down(give, 1, 0.0), jnp.where(part == 1, give, jnp.where(part == 2, rows_up(give, 1, 0.0), 0.0))
    )

    bytes_of(row_all.at[pl.ds(0, n_slab - 1)], row_sem).wait()
    corr = jnp.sum(line_w[...] * row_all[...].reshape(n_slab, 128), axis=0, keepdims=True)
    corr = corr + pltpu.roll(corr, 128 - 8, 1)
    corr = corr + pltpu.roll(corr, 128 - 16, 1) + pltpu.roll(corr, 128 - 32, 1)
    corr = jnp.broadcast_to(corr, (8, 128))
    results = []
    for v in range(4):
        cell = row8(cells, 0, v)
        lift = lanes(corr, (cell >> 3) * 64 + (cell & 7))
        at = pl.ds(128 * v, 128)
        for t in range(8):
            base[pl.ds(8 * t, 8), at] = gath[pl.ds(8 * t, 8), at] + lift
        results.append(pltpu.make_async_copy(base.at[:, at], out_hbm.at[:, at], out_sem.at[v]))
        results[v].start()

    for copy in copies[0] + copies[1] + infos:
        copy.wait_send()
    bytes_of(line_all.at[pl.ds(0, n_slab - 1)], send_sem.at[24]).wait()
    bytes_of(mix_all.at[pl.ds(0, n_col - 1)], send_sem.at[25]).wait()
    bytes_of(row_all.at[pl.ds(0, n_slab - 1)], send_sem.at[26]).wait()
    for result in results:
        result.wait()


def solution(mesh):
    n_slab, n_col = mesh.shape["slab"], mesh.shape["col"]
    stack, sums, weights, centre = tables(n_col)

    def shards(rhs, start, screen, neighbours, col_send, slab_send, coarse_map, coupling, coarse_scale):
        hbm = pl.BlockSpec(memory_space=pltpu.HBM)
        vmem = pltpu.VMEM
        dma = pltpu.SemaphoreType.DMA
        return pl.pallas_call(
            functools.partial(kernel, n_slab, n_col, centre),
            out_shape=jax.ShapeDtypeStruct((64, NB), F32),
            in_specs=[hbm] * 12,
            out_specs=hbm,
            scratch_shapes=[
                vmem((64, NB), F32),
                vmem((64, NB), F32),
                vmem((64, NB), F32),
                vmem((27, NB), I32),
                vmem((2, FCOL), I32),
                vmem((2, FSLAB), I32),
                vmem((1, NB), I32),
                pltpu.SMEM((2, 2, 4), F32),
                pltpu.SMEM((2, 2, 4), F32),
                vmem((128, 512), BF16),
                vmem((64, 64), BF16),
                vmem((n_col, 8, 128), F32),
                vmem((512, NB), F32),
                vmem((2, 384, 256), F32),
                vmem((64, NB), F32),
                vmem((32, NB), I32),
                vmem((2, 4, 2, 8, 128), F32),
                vmem((2, 4, 2, 8, 128), F32),
                vmem((2, 4, 2, 8, 128), F32),
                vmem((2, 4, 2, 8, 128), F32),
                vmem((2, 4, 2, 8, 128), F32),
                vmem((2, 8, 256), I32),
                vmem((2, 8, 128), I32),
                vmem((2, 8, 256), I32),
                vmem((2, 8, 128), I32),
                vmem((2, 2, 8, 128), I32),
                vmem((32, NB), I32),
                vmem((8, 128), F32),
                vmem((n_slab, 1, 128), F32),
                vmem((n_slab, 128), F32),
                vmem((n_col, 8, 128), F32),
                vmem((8, 128), F32),
                vmem((1, 128), F32),
                vmem((n_slab, 1, 128), F32),
                dma((12,)),
                dma((4,)),
                dma((27,)),
                dma((16,)),
                dma((8,)),
                dma,
                dma,
                dma,
                pltpu.SemaphoreType.REGULAR((4,)),
            ],
            compiler_params=pltpu.CompilerParams(
                collective_id=0, has_side_effects=True, vmem_limit_bytes=63 * 1024 * 1024
            ),
            cost_estimate=pl.CostEstimate(flops=10**8, bytes_accessed=10**6, transcendentals=0),
        )(
            rhs, start, screen, neighbours, col_send, slab_send,
            coarse_map.reshape(1, NB), coupling, coarse_scale,
            jnp.asarray(stack), jnp.asarray(sums), jnp.asarray(weights),
        )

    block = P(None, ("slab", "col"))
    line = P("slab", "col", None)
    placed = (block,) * 6 + (P(("slab", "col")), line, line)
    return jax.shard_map(shards, mesh=mesh, in_specs=placed, out_specs=block, check_vma=False)
```

```python
import functools

import jax
import jax.numpy as jnp
import numpy as np
from jax import lax
from jax.experimental import pallas as pl
from jax.experimental.pallas import tpu as pltpu
from jax.sharding import PartitionSpec as P

MESH = pl.DeviceIdType.MESH
F32 = jnp.float32
BF16 = jnp.bfloat16
I32 = jnp.int32
NB = 512
FCOL = 128
FSLAB = 160
RELAX = 0.5
COL0 = NB + 1
SLAB_LOW = COL0 + 2 * FCOL
SLAB_HIGH = SLAB_LOW + FSLAB
AT_CL, AT_CH, AT_SLAB, AT_DL, AT_DH, AT_NONE = 5, 6, 10, 11, 12, 13
BLOCKS = (0, 1, 4, 5, 2, 3, 6, 7)
NOWHERE = -1000


def stencil_table():
    masses = np.array([11.0 / 20.0, 13.0 / 60.0, 1.0 / 120.0])
    slopes = np.array([1.0, -1.0 / 3.0, -1.0 / 6.0])
    coeffs = np.arange(64)
    along = (coeffs // 16, coeffs // 4 % 4, coeffs % 4)
    offsets = np.arange(27)
    shift = (offsets // 9 - 1, offsets // 3 % 3 - 1, offsets % 3 - 1)
    dist = [
        4 * shift[k][None, :, None] + along[k][None, None, :] - along[k][:, None, None]
        for k in range(3)
    ]
    inside = (np.abs(dist[0]) <= 2) & (np.abs(dist[1]) <= 2) & (np.abs(dist[2]) <= 2)
    m = [masses[np.minimum(np.abs(d), 2)] for d in dist]
    s = [slopes[np.minimum(np.abs(d), 2)] for d in dist]
    values = s[0] * m[1] * m[2] + m[0] * s[1] * m[2] + m[0] * m[1] * s[2]
    return np.where(inside, values, 0.0)


def split_np(x):
    x = np.asarray(x, np.float32)
    high = x.astype(jnp.bfloat16)
    return high, (x - high.astype(np.float32)).astype(jnp.bfloat16)


def tables(n_col):
    stencil = stencil_table()
    packed = np.zeros((64, 512))
    for at, blk in enumerate(BLOCKS):
        sx, sy, sz = blk // 4, blk // 2 % 2, blk % 2
        for j in range(64):
            a, b, e = j // 16, j // 4 % 4, j % 4
            dx = sx * (1 if a < 2 else -1)
            dy = sy * (1 if b < 2 else -1)
            dz = sz * (1 if e < 2 else -1)
            packed[:, at * 64 + j] = stencil[:, 9 * (dx + 1) + 3 * (dy + 1) + dz + 1, j]
    stack = np.concatenate(split_np(packed), 0)
    sums = np.zeros((32, 64))
    for o in range(27):
        sums[o] = stencil[:, 26 - o, :].sum(0)
    sums_stack = np.concatenate(split_np(sums), 0)
    rows = 2 * n_col
    ymatrix = 2.5 * np.eye(rows) - np.eye(rows, k=1) - np.eye(rows, k=-1)
    inverse = np.linalg.inv(ymatrix)
    weights = np.zeros((n_col, n_col, 8, 128), np.float32)
    for own in range(n_col):
        for src in range(n_col):
            for dc in range(3):
                c = src + dc - 1
                if not 0 <= c < n_col:
                    continue
                for lane in range(128):
                    k = lane % 64
                    if k >= 48:
                        continue
                    y = k // 4 % 2
                    y_src = y if lane < 64 else 1 - y
                    weights[own, src, dc, lane] = inverse[2 * own + y, 2 * c + y_src]
    return stack, sums_stack, weights, float(np.float32(stencil[0, 13, 0]))


def split(x):
    high = x.astype(BF16)
    return high, (x - high.astype(F32)).astype(BF16)


def lanes(x, index):
    return jnp.take_along_axis(x, index, axis=1, mode="promise_in_bounds")


def own_sources(v, dx, dy):
    if dx == 1:
        span = range(v, v + 3)
    elif dx == -1:
        span = range(v - 2, v + 1)
    elif dy == 1:
        span = range(v, v + 2)
    elif dy == -1:
        span = range(v - 1, v + 1)
    else:
        span = range(v - 1, v + 2)
    return [w for w in span if 0 <= w < 4]


def kernel(
    n_slab, n_col, centre,
    rhs_hbm, start_hbm, screen_hbm, nbr_hbm, colsend_hbm, slabsend_hbm, cells_hbm, coupling_hbm, scale_hbm,
    stack_hbm, sums_hbm, weights_hbm,
    out_hbm,
    rhs, screen, step, nbr, colsend, slabsend, cells, coupling_ref, scale_ref, stack, sums, weights,
    gath, edge, base, nbn, fc, fs, rc, rs, diag, info_s, info_c, in_s, in_c, in_d,
    codes, line_own, line_all, line_w, mix_all, mix_own, row_own, row_all,
    load_sem, out_sem, send_sem, halo_sem, info_sem, line_sem, mix_sem, row_sem, far_sem,
):
    s = lax.axis_index("slab")
    c = lax.axis_index("col")
    s_up, s_dn = lax.rem(s + 1, n_slab), lax.rem(s + n_slab - 1, n_slab)
    c_up, c_dn = lax.rem(c + 1, n_col), lax.rem(c + n_col - 1, n_col)

    barrier = pltpu.get_barrier_semaphore()

    def hello(device):
        pl.semaphore_signal(barrier, inc=1, device_id=device, device_id_type=MESH)

    near = 4 if n_slab >= 32 else 1
    for device in ((s_up, c_up), (s_up, c_dn), (s_dn, c_up), (s_dn, c_dn)):
        hello(device)
    for d in range(1, near + 1):
        hello((lax.rem(s + d, n_slab), c))
        hello((lax.rem(s + n_slab - d, n_slab), c))
    hello((s, c_up))
    hello((s, c_dn))

    loads = [
        pltpu.make_async_copy(a, b, load_sem.at[k])
        for k, (a, b) in enumerate([
            (start_hbm, gath.at[pl.ds(0, 64)]),
            (colsend_hbm, colsend),
            (slabsend_hbm, slabsend),
            (cells_hbm, cells),
            (coupling_hbm, coupling_ref),
            (scale_hbm, scale_ref),
            (nbr_hbm, nbr),
            (screen_hbm, screen),
            (rhs_hbm, rhs),
            (stack_hbm, stack),
            (sums_hbm, sums),
            (weights_hbm.at[c], weights),
        ])
    ]
    for load in loads:
        load.start()

    sub = lax.broadcasted_iota(I32, (8, 128), 0)
    lane = lax.broadcasted_iota(I32, (8, 128), 1)
    e_low = lax.rem(sub, 4) < 2

    def row8(ref, r, v):
        return jnp.broadcast_to(ref[pl.ds(r, 1), pl.ds(128 * v, 128)], (8, 128))

    for load in loads[:6]:
        load.wait()

    col_index = [row8(colsend, k, 0) for k in range(2)]
    beyond = jnp.full((1, 256 - FSLAB), NB)
    slab_index = [
        [
            row8(slabsend, k, 0),
            jnp.broadcast_to(jnp.concatenate([slabsend[pl.ds(k, 1), pl.ds(128, FSLAB - 128)], beyond], axis=1), (8, 128)),
        ]
        for k in range(2)
    ]

    line_row = jnp.zeros((8, 128), F32)
    for k in range(16):
        line_row = jnp.where(lane == k, coupling_ref[k // 8, k // 4 % 2, k % 4], line_row)
        line_row = jnp.where(lane == 16 + k, scale_ref[k // 8, k // 4 % 2, k % 4], line_row)
    line_own[...] = line_row

    def pick(index, source, spans, empty):
        low, high = index & 127, index >> 7
        got = jnp.full((8, 128), empty)
        for v in spans:
            got = jnp.where(high == v, lanes(source(v), low), got)
        return got

    def faces(k):
        for a in range(4):
            for bh in range(2):
                t = 2 * a + bh
                source = lambda v: gath[pl.ds(8 * t, 8), pl.ds(128 * v, 128)]
                fs[k, a, bh] = source(0 if a < 2 else 3)
                fc[k, a, bh] = pick(col_index[0 if bh == 0 else 1], source, range(4), 0.0)

    faces(0)
    cell_source = lambda v: row8(cells, 0, v)
    for k in range(2):
        info_c[k] = pick(col_index[k], cell_source, range(4), NOWHERE)
        for w in range(2):
            info_s[k, :, pl.ds(128 * w, 128)] = jnp.where(sub == 0, slab_index[k][w], cell_source(3 * k))

    pl.semaphore_wait(barrier, 6 + 2 * near)

    reaches = []
    while near < n_slab // 2:
        reaches.append(near)
        near *= 2

    def tell(k):
        if k < len(reaches):
            for d in (reaches[k], n_slab - reaches[k]):
                pl.semaphore_signal(
                    far_sem.at[k], inc=1, device_id=(lax.rem(s + d, n_slab), c), device_id_type=MESH
                )

    def hear(k):
        if k < len(reaches):
            pl.semaphore_wait(far_sem.at[k], 2)

    across_far = n_col > 4

    tell(0)

    def send(src, dst, sent, recv, device):
        copy = pltpu.make_async_remote_copy(
            src_ref=src, dst_ref=dst, send_sem=sent, recv_sem=recv, device_id=device, device_id_type=MESH
        )
        copy.start()
        return copy

    low2, high2 = pl.ds(0, 2), pl.ds(2, 2)

    def send_faces(k):
        return [
            send(src, dst, send_sem.at[8 * k + m], halo_sem.at[8 * k + m], device)
            for m, (src, dst, device) in enumerate([
                (fc.at[k, low2, 0], diag.at[k, low2, 0], (s_dn, c_dn)),
                (fc.at[k, low2, 1], diag.at[k, low2, 1], (s_dn, c_up)),
                (fc.at[k, high2, 0], diag.at[k, high2, 0], (s_up, c_dn)),
                (fc.at[k, high2, 1], diag.at[k, high2, 1], (s_up, c_up)),
                (fs.at[k, low2], rs.at[k, low2], (s_dn, c)),
                (fs.at[k, high2], rs.at[k, high2], (s_up, c)),
                (fc.at[k, :, 0], rc.at[k, :, 0], (s, c_dn)),
                (fc.at[k, :, 1], rc.at[k, :, 1], (s, c_up)),
            ])
        ]

    def bytes_of(ref, sem):
        return pltpu.make_async_copy(ref, ref, sem)

    copies = [send_faces(0)]
    infos = [
        send(src, dst, send_sem.at[16 + m], info_sem.at[m], device)
        for m, (src, dst, device) in enumerate([
            (info_s.at[0], in_s.at[0], (s_dn, c)),
            (info_s.at[1], in_s.at[1], (s_up, c)),
            (info_c.at[0], in_c.at[0], (s, c_dn)),
            (info_c.at[1], in_c.at[1], (s, c_up)),
            (info_c.at[0], in_d.at[0, 0], (s_dn, c_dn)),
            (info_c.at[1], in_d.at[0, 1], (s_dn, c_up)),
            (info_c.at[0], in_d.at[1, 0], (s_up, c_dn)),
            (info_c.at[1], in_d.at[1, 1], (s_up, c_up)),
        ])
    ]
    for load in loads[6:]:
        load.wait()

    def place(there, at):
        return 128 * jnp.where(there, at, AT_NONE)

    above, below, right, left = s < n_slab - 1, s > 0, c < n_col - 1, c > 0

    def raw_rows(r, v):
        if r < 3:
            return nbr[pl.ds(8 * r, 8), pl.ds(128 * v, 128)]
        index = jnp.full((8, 128), NB)
        for k in range(3):
            index = jnp.where(sub == k, row8(nbr, 24 + k, v), index)
        return index

    def place_col(index):
        at = index - COL0
        got = jnp.where(index < NB, index, 128 * AT_NONE)
        got = jnp.where((at >> 7) == 0, place(left, AT_CL) + (at & 127), got)
        return jnp.where((at >> 7) == 1, place(right, AT_CH) + (at & 127), got)

    def place_slab(index, got, up):
        at = index - (SLAB_HIGH if up else SLAB_LOW)
        side, there = (0, above) if up else (1, below)
        listed = jnp.full((8, 128), NB)
        for w in range(2):
            table = jnp.broadcast_to(in_s[side, pl.ds(0, 1), pl.ds(128 * w, 128)], (8, 128))
            listed = jnp.where((at >> 7) == w, lanes(table, at & 127), listed)
        col = listed - COL0
        spot = jnp.where((listed >> 7) == (0 if up else 3), place(there, AT_SLAB) + (listed & 127), 128 * AT_NONE)
        spot = jnp.where((col >> 7) == 0, place(there & left, AT_DL) + (col & 127), spot)
        spot = jnp.where((col >> 7) == 1, place(there & right, AT_DH) + (col & 127), spot)
        return jnp.where((at >= 0) & (at < FSLAB), spot, got)

    def pattern(dx, dy, sz, v):
        o = 9 * (dx + 1) + 3 * (dy + 1) + 1
        if sz == 0:
            return row8(nbn, o, v)
        return jnp.where(e_low, row8(nbn, o + 1, v), row8(nbn, o - 1, v))

    def groups(v):
        for at, blk in enumerate(BLOCKS):
            if blk == 0:
                continue
            sx, sy, sz = blk // 4, blk // 2 % 2, blk % 2
            for dx in ((1, -1) if sx else (0,)):
                for dy in ((1, -1) if sy else (0,)):
                    halves = range(4) if dx == 0 else ((0, 1) if dx == 1 else (2, 3))
                    bhs = (0, 1) if dy == 0 else ((0,) if dy == 1 else (1,))
                    yield at, dx, dy, sz, [2 * a + bh for a in halves for bh in bhs]

    def gather_own():
        for v in range(4):
            for blk, dx, dy, sz, rows in groups(v):
                index = pattern(dx, dy, sz, v)
                low, high = index & 127, index >> 7
                spans = own_sources(v, dx, dy)
                masks = {w: high == w for w in spans}
                for t in rows:
                    got = jnp.zeros((8, 128), F32)
                    for w in spans:
                        got = jnp.where(masks[w], lanes(gath[pl.ds(8 * t, 8), pl.ds(128 * w, 128)], low), got)
                    gath[pl.ds(64 * blk + 8 * t, 8), pl.ds(128 * v, 128)] = got

    def gather_rims(k, v, slot, half, along):
        for blk, dx, dy, sz, rows in groups(v):
            if along and not ((dx == 1 and v == 3) or (dx == -1 and v == 0)):
                continue
            if dy == 0 and not along:
                continue
            index = pattern(dx, dy, sz, v)
            low, high = index & 127, index >> 7
            for t in rows:
                a, bh = t // 2, t % 2
                at = (half, pl.ds(64 * (blk - 2) + 8 * t, 8), pl.ds(128 * slot, 128))
                got = edge[at] if along and dy else jnp.zeros((8, 128), F32)
                if along:
                    got = jnp.where(high == AT_SLAB, lanes(rs[k, a, bh], low), got)
                    if dy:
                        got = jnp.where(high == (AT_DH if dy == 1 else AT_DL), lanes(diag[k, a, bh], low), got)
                else:
                    got = jnp.where(high == (AT_CH if dy == 1 else AT_CL), lanes(rc[k, a, bh], low), got)
                edge[at] = got

    def product(source, rows):
        high, low = split(source)
        both = jnp.dot(stack[:, rows], high, preferred_element_type=F32)
        return both[:64] + both[64:] + jnp.dot(stack[pl.ds(0, 64), rows], low, preferred_element_type=F32)

    def sweep_own():
        gather_own()
        field = gath[pl.ds(0, 64)]
        total = product(gath[...], pl.ds(0, 512))
        base[...] = field + step[...] * (rhs[...] - total - screen[...] * field)

    def finish(half, vs):
        first = 256 if half == 0 else 128
        total = product(edge[half, pl.ds(first - 128, 512 - first)], pl.ds(first, 512 - first))
        for slot, v in enumerate(vs):
            at = pl.ds(128 * v, 128)
            gath[pl.ds(0, 64), at] = base[:, at] - step[:, at] * total[:, 128 * slot : 128 * slot + 128]

    def sweep_rims(k, meanwhile):
        for copy in copies[k][6:]:
            copy.wait_recv()
        for slot, v in enumerate((1, 2)):
            gather_rims(k, v, slot, 0, False)
        finish(0, (1, 2))
        for slot, v in enumerate((0, 3)):
            gather_rims(k, v, slot, 1, False)
        meanwhile()
        for copy in copies[k][:6]:
            copy.wait_recv()
        for slot, v in enumerate((0, 3)):
            gather_rims(k, v, slot, 1, True)
        finish(1, (0, 3))

    step[...] = RELAX / (centre + screen[...])
    edge[1, pl.ds(0, 128)] = jnp.zeros((128, 256), F32)
    for r in range(4):
        for v in range(4):
            nbn[pl.ds(8 * r, 8), pl.ds(128 * v, 128)] = place_col(raw_rows(r, v))
    sweep_own()

    def after_first():
        hear(0)
        tell(1)
        if across_far:
            for d in (2, n_col - 2):
                pl.semaphore_signal(far_sem.at[3], inc=1, device_id=(s, lax.rem(c + d, n_col)), device_id_type=MESH)
        for copy in infos[:2]:
            copy.wait_recv()
        for r in range(4):
            at = (pl.ds(8 * r, 8), pl.ds(0 if r < 2 else 384, 128))
            nbn[at] = place_slab(raw_rows(r, 0 if r < 2 else 3), nbn[at], r >= 2)

    def after_second():
        hear(1)
        tell(2)

    sweep_rims(0, after_first)
    faces(1)
    copies.append(send_faces(1))
    sweep_own()

    for copy in infos[2:]:
        copy.wait_recv()
    own_codes = [row8(cells, 0, v) + 64 for v in range(4)]
    col_codes = [in_c[1] + 48, in_c[0] + 80]
    for r in range(4):
        for v in range(4):
            index = nbn[pl.ds(8 * r, 8), pl.ds(128 * v, 128)]
            low, high = index & 127, index >> 7
            code = jnp.full((8, 128), NOWHERE)
            for w in range(4):
                code = jnp.where(high == w, lanes(own_codes[w], low), code)
            for w, at in enumerate((AT_CL, AT_CH)):
                code = jnp.where(high == at, lanes(col_codes[w], low), code)
            if (r < 2 and v == 0) or (r >= 2 and v == 3):
                side, first = (1, 0) if r < 2 else (0, 96)
                beside = jnp.broadcast_to(in_s[side, pl.ds(1, 1), pl.ds(0, 128)], (8, 128))
                code = jnp.where(high == AT_SLAB, lanes(beside, low) + first + 16, code)
                code = jnp.where(high == AT_DL, lanes(in_d[side, 1], low) + first, code)
                code = jnp.where(high == AT_DH, lanes(in_d[side, 0], low) + first + 32, code)
            codes[pl.ds(8 * r, 8), pl.ds(128 * v, 128)] = code

    sweep_rims(1, after_second)
    field = gath[pl.ds(0, 64)]

    high, low = split(field)
    both = jnp.dot(sums[...], high, preferred_element_type=F32)
    given = both[:32] + both[32:] + jnp.dot(sums[pl.ds(0, 32)], low, preferred_element_type=F32)
    local = jnp.sum(rhs[...] - screen[...] * field, axis=0, keepdims=True)
    row_at = lax.broadcasted_iota(I32, (32, 512), 0)
    given = (jnp.where(row_at == 13, jnp.broadcast_to(local, (32, 512)), 0.0) - given) * (1.0 / 64.0)

    def fold(parts):
        for bit in (4, 2, 1):
            keep = (sub & bit) == 0
            merged = []
            for k in range(bit):
                one, two = parts[k], parts[k + bit]
                stay, go = jnp.where(keep, one, two), jnp.where(keep, two, one)
                if bit == 4:
                    merged.append(stay + pltpu.roll(go, 4, 0))
                else:
                    merged.append(stay + jnp.where(keep, pltpu.roll(go, 8 - bit, 0), pltpu.roll(go, bit, 0)))
            parts = merged
        return parts[0]

    reach = {
        (0, 0): ((0, 1, 2, 3), range(4)),
        (0, -1): ((0, 1, 2), range(4)),
        (0, 1): ((0, 1, 2, 3), range(4)),
        (-1, 0): ((0, 1), (0,)),
        (-1, -1): ((0,), (0,)),
        (-1, 1): ((0, 1), (0,)),
        (1, 0): ((2, 3), (3,)),
        (1, -1): ((2,), (3,)),
        (1, 1): ((3,), (3,)),
    }
    nought = jnp.zeros((8, 128), F32)
    stacked = []
    for dc in (-1, 0, 1):
        plain, swapped = [], []
        for ds in (-1, 0, 1):
            rs_of, vs_of = reach[(ds, dc)]
            first_code = 48 * (ds + 1) + 16 * (dc + 1)
            for x in range(2):
                parts = []
                for k in range(8):
                    acc = nought
                    for r in rs_of:
                        for v in vs_of:
                            hit = codes[pl.ds(8 * r, 8), pl.ds(128 * v, 128)] == first_code + 8 * x + k
                            acc = acc + jnp.where(hit, given[8 * r : 8 * r + 8, 128 * v : 128 * v + 128], 0.0)
                    parts.append(acc)
                total = fold(parts)
                plain.append(total)
                swapped.append(pltpu.roll(total, 4, 0))
        stacked += plain + [nought, nought] + swapped + [nought, nought]
    high, low = split(jnp.concatenate(stacked, axis=0))
    ones = jnp.ones((16, 128), BF16)
    across = (((1,), (1,)), ((), ()))
    summed = lax.dot_general(ones, high, across, preferred_element_type=F32) + lax.dot_general(
        ones, low, across, preferred_element_type=F32
    )
    message = jnp.where(
        sub == 0, summed[:8, :128], jnp.where(sub == 1, summed[:8, 128:256], jnp.where(sub == 2, summed[:8, 256:], 0.0))
    )
    if across_far:
        pl.semaphore_wait(far_sem.at[3], 2)
    mix_own[...] = message
    mix_all[pl.ds(c, 1)] = message.reshape(1, 8, 128)

    @pl.loop(1, n_col)
    def _(d):
        send(mix_own, mix_all.at[c], send_sem.at[25], mix_sem, (s, lax.rem(c + d, n_col)))

    hear(2)
    line_all[pl.ds(s, 1)] = line_own[pl.ds(0, 1)].reshape(1, 1, 128)

    @pl.loop(1, n_slab)
    def _(d):
        send(line_own.at[pl.ds(0, 1)], line_all.at[s], send_sem.at[24], line_sem, (lax.rem(s + d, n_slab), c))

    bytes_of(mix_all.at[pl.ds(0, n_col - 1)], mix_sem).wait()
    mixed = jnp.zeros((8, 128), F32)
    for k in range(n_col):
        mixed = mixed + weights[k] * mix_all[k]
    row = jnp.sum(mixed, axis=0, keepdims=True)
    row = row + pltpu.roll(row, 64, 1)
    row_own[...] = row
    row_all[pl.ds(s, 1)] = row.reshape(1, 1, 128)

    @pl.loop(1, n_slab, unroll=9 if n_slab == 64 else 1)
    def _(d):
        send(row_own, row_all.at[s], send_sem.at[26], row_sem, (lax.rem(s + d, n_slab), c))

    bytes_of(line_all.at[pl.ds(0, n_slab - 1)], line_sem).wait()
    all_rows = line_all[...].reshape(n_slab, 128)
    big_lane = lax.broadcasted_iota(I32, (n_slab, 128), 1)
    big_row = lax.broadcasted_iota(I32, (n_slab, 128), 0)
    spot = big_lane & 7
    c0, c1, p0, p1 = [lanes(all_rows, spot + 8 * k) for k in range(4)]
    first = big_lane < 64
    after, here = big_row > s, big_row == s

    def rows_down(x, d, fill):
        return jnp.where(big_row >= d, pltpu.roll(x, d, 0), fill)

    def rows_up(x, d, fill):
        return jnp.where(big_row < n_slab - d, pltpu.roll(x, n_slab - d, 0), fill)

    run = jnp.where(after, c0 * c1, jnp.where(here, jnp.where(first, c0 * c1, c1), 1.0))
    d = 1
    while d < n_slab:
        run = run * rows_down(run, d, 1.0)
        d *= 2
    run = rows_down(run, 1, 1.0)
    w0 = jnp.where(after, run, jnp.where(here & first, 1.0, 0.0))
    w1 = jnp.where(after, run * c0, jnp.where(here, jnp.where(first, c0, 1.0), 0.0))
    u0, u1 = p0 * w0, p1 * w1
    c0_next = rows_up(c0, 1, 0.0)
    tail, factor = u0 + c1 * u1, c1 * c0_next
    d = 1
    while d < n_slab:
        tail = tail + factor * rows_up(tail, d, 0.0)
        factor = factor * rows_up(factor, d, 0.0)
        d *= 2
    second = u1 + c0_next * rows_up(tail, 1, 0.0)
    give = jnp.where((big_lane & 8) == 0, tail, second)
    part = (big_lane & 63) >> 4
    line_w[...] = jnp.where(
        part == 0, rows_down(give, 1, 0.0), jnp.where(part == 1, give, jnp.where(part == 2, rows_up(give, 1, 0.0), 0.0))
    )

    bytes_of(row_all.at[pl.ds(0, n_slab - 1)], row_sem).wait()
    corr = jnp.sum(line_w[...] * row_all[...].reshape(n_slab, 128), axis=0, keepdims=True)
    corr = corr + pltpu.roll(corr, 128 - 8, 1)
    corr = corr + pltpu.roll(corr, 128 - 16, 1) + pltpu.roll(corr, 128 - 32, 1)
    corr = jnp.broadcast_to(corr, (8, 128))
    results = []
    for v in range(4):
        cell = row8(cells, 0, v)
        lift = lanes(corr, (cell >> 3) * 64 + (cell & 7))
        at = pl.ds(128 * v, 128)
        for t in range(8):
            base[pl.ds(8 * t, 8), at] = gath[pl.ds(8 * t, 8), at] + lift
        results.append(pltpu.make_async_copy(base.at[:, at], out_hbm.at[:, at], out_sem.at[v]))
        results[v].start()

    for copy in copies[0] + copies[1] + infos:
        copy.wait_send()
    bytes_of(line_all.at[pl.ds(0, n_slab - 1)], send_sem.at[24]).wait()
    bytes_of(mix_all.at[pl.ds(0, n_col - 1)], send_sem.at[25]).wait()
    bytes_of(row_all.at[pl.ds(0, n_slab - 1)], send_sem.at[26]).wait()
    for result in results:
        result.wait()


def solution(mesh):
    n_slab, n_col = mesh.shape["slab"], mesh.shape["col"]
    stack, sums, weights, centre = tables(n_col)

    def shards(rhs, start, screen, neighbours, col_send, slab_send, coarse_map, coupling, coarse_scale):
        hbm = pl.BlockSpec(memory_space=pltpu.HBM)
        vmem = pltpu.VMEM
        dma = pltpu.SemaphoreType.DMA
        return pl.pallas_call(
            functools.partial(kernel, n_slab, n_col, centre),
            out_shape=jax.ShapeDtypeStruct((64, NB), F32),
            in_specs=[hbm] * 12,
            out_specs=hbm,
            scratch_shapes=[
                vmem((64, NB), F32),
                vmem((64, NB), F32),
                vmem((64, NB), F32),
                vmem((27, NB), I32),
                vmem((2, FCOL), I32),
                vmem((2, FSLAB), I32),
                vmem((1, NB), I32),
                pltpu.SMEM((2, 2, 4), F32),
                pltpu.SMEM((2, 2, 4), F32),
                vmem((128, 512), BF16),
                vmem((64, 64), BF16),
                vmem((n_col, 8, 128), F32),
                vmem((512, NB), F32),
                vmem((2, 384, 256), F32),
                vmem((64, NB), F32),
                vmem((32, NB), I32),
                vmem((2, 4, 2, 8, 128), F32),
                vmem((2, 4, 2, 8, 128), F32),
                vmem((2, 4, 2, 8, 128), F32),
                vmem((2, 4, 2, 8, 128), F32),
                vmem((2, 4, 2, 8, 128), F32),
                vmem((2, 8, 256), I32),
                vmem((2, 8, 128), I32),
                vmem((2, 8, 256), I32),
                vmem((2, 8, 128), I32),
                vmem((2, 2, 8, 128), I32),
                vmem((32, NB), I32),
                vmem((8, 128), F32),
                vmem((n_slab, 1, 128), F32),
                vmem((n_slab, 128), F32),
                vmem((n_col, 8, 128), F32),
                vmem((8, 128), F32),
                vmem((1, 128), F32),
                vmem((n_slab, 1, 128), F32),
                dma((12,)),
                dma((4,)),
                dma((27,)),
                dma((16,)),
                dma((8,)),
                dma,
                dma,
                dma,
                pltpu.SemaphoreType.REGULAR((4,)),
            ],
            compiler_params=pltpu.CompilerParams(
                collective_id=0, has_side_effects=True, vmem_limit_bytes=63 * 1024 * 1024
            ),
            cost_estimate=pl.CostEstimate(flops=10**8, bytes_accessed=10**6, transcendentals=0),
        )(
            rhs, start, screen, neighbours, col_send, slab_send,
            coarse_map.reshape(1, NB), coupling, coarse_scale,
            jnp.asarray(stack), jnp.asarray(sums), jnp.asarray(weights),
        )

    block = P(None, ("slab", "col"))
    line = P("slab", "col", None)
    placed = (block,) * 6 + (P(("slab", "col")), line, line)
    return jax.shard_map(shards, mesh=mesh, in_specs=placed, out_specs=block, check_vma=False)
```

```python
import functools

import jax
import jax.numpy as jnp
import numpy as np
from jax import lax
from jax.experimental import pallas as pl
from jax.experimental.pallas import tpu as pltpu
from jax.sharding import PartitionSpec as P

MESH = pl.DeviceIdType.MESH
F32 = jnp.float32
BF16 = jnp.bfloat16
I32 = jnp.int32
NB = 512
FCOL = 128
FSLAB = 160
RELAX = 0.5
COL0 = NB + 1
SLAB_LOW = COL0 + 2 * FCOL
SLAB_HIGH = SLAB_LOW + FSLAB
AT_CL, AT_CH, AT_SLAB, AT_DL, AT_DH, AT_NONE = 5, 6, 10, 11, 12, 13
BLOCKS = (0, 1, 4, 5, 2, 3, 6, 7)
NOWHERE = -1000


def stencil_table():
    masses = np.array([11.0 / 20.0, 13.0 / 60.0, 1.0 / 120.0])
    slopes = np.array([1.0, -1.0 / 3.0, -1.0 / 6.0])
    coeffs = np.arange(64)
    along = (coeffs // 16, coeffs // 4 % 4, coeffs % 4)
    offsets = np.arange(27)
    shift = (offsets // 9 - 1, offsets // 3 % 3 - 1, offsets % 3 - 1)
    dist = [
        4 * shift[k][None, :, None] + along[k][None, None, :] - along[k][:, None, None]
        for k in range(3)
    ]
    inside = (np.abs(dist[0]) <= 2) & (np.abs(dist[1]) <= 2) & (np.abs(dist[2]) <= 2)
    m = [masses[np.minimum(np.abs(d), 2)] for d in dist]
    s = [slopes[np.minimum(np.abs(d), 2)] for d in dist]
    values = s[0] * m[1] * m[2] + m[0] * s[1] * m[2] + m[0] * m[1] * s[2]
    return np.where(inside, values, 0.0)


def split_np(x):
    x = np.asarray(x, np.float32)
    high = x.astype(jnp.bfloat16)
    return high, (x - high.astype(np.float32)).astype(jnp.bfloat16)


def tables(n_col):
    stencil = stencil_table()
    packed = np.zeros((64, 512))
    for at, blk in enumerate(BLOCKS):
        sx, sy, sz = blk // 4, blk // 2 % 2, blk % 2
        for j in range(64):
            a, b, e = j // 16, j // 4 % 4, j % 4
            dx = sx * (1 if a < 2 else -1)
            dy = sy * (1 if b < 2 else -1)
            dz = sz * (1 if e < 2 else -1)
            packed[:, at * 64 + j] = stencil[:, 9 * (dx + 1) + 3 * (dy + 1) + dz + 1, j]
    stack = np.concatenate(split_np(packed), 0)
    sums = np.zeros((32, 64))
    for o in range(27):
        sums[o] = stencil[:, 26 - o, :].sum(0)
    sums_stack = np.concatenate(split_np(sums), 0)
    rows = 2 * n_col
    ymatrix = 2.5 * np.eye(rows) - np.eye(rows, k=1) - np.eye(rows, k=-1)
    inverse = np.linalg.inv(ymatrix)
    weights = np.zeros((n_col, n_col, 8, 128), np.float32)
    for own in range(n_col):
        for src in range(n_col):
            for dc in range(3):
                c = src + dc - 1
                if not 0 <= c < n_col:
                    continue
                for lane in range(128):
                    k = lane % 64
                    if k >= 48:
                        continue
                    y = k // 4 % 2
                    y_src = y if lane < 64 else 1 - y
                    weights[own, src, dc, lane] = inverse[2 * own + y, 2 * c + y_src]
    return stack, sums_stack, weights, float(np.float32(stencil[0, 13, 0]))


def split(x):
    high = x.astype(BF16)
    return high, (x - high.astype(F32)).astype(BF16)


def lanes(x, index):
    return jnp.take_along_axis(x, index, axis=1, mode="promise_in_bounds")


def own_sources(v, dx, dy):
    if dx == 1:
        span = range(v, v + 3)
    elif dx == -1:
        span = range(v - 2, v + 1)
    elif dy == 1:
        span = range(v, v + 2)
    elif dy == -1:
        span = range(v - 1, v + 1)
    else:
        span = range(v - 1, v + 2)
    return [w for w in span if 0 <= w < 4]


def kernel(
    n_slab, n_col, centre,
    rhs_hbm, start_hbm, screen_hbm, nbr_hbm, colsend_hbm, slabsend_hbm, cells_hbm, coupling_hbm, scale_hbm,
    stack_hbm, sums_hbm, weights_hbm,
    out_hbm,
    rhs, screen, step, nbr, colsend, slabsend, cells, coupling_ref, scale_ref, stack, sums, weights,
    gath, edge, base, nbn, fc, fs, rc, rs, diag, info_s, info_c, in_s, in_c, in_d,
    codes, line_own, line_all, line_w, mix_all, mix_own, row_own, row_all,
    load_sem, out_sem, send_sem, halo_sem, info_sem, line_sem, mix_sem, row_sem, far_sem,
):
    s = lax.axis_index("slab")
    c = lax.axis_index("col")
    s_up, s_dn = lax.rem(s + 1, n_slab), lax.rem(s + n_slab - 1, n_slab)
    c_up, c_dn = lax.rem(c + 1, n_col), lax.rem(c + n_col - 1, n_col)

    barrier = pltpu.get_barrier_semaphore()

    def hello(device):
        pl.semaphore_signal(barrier, inc=1, device_id=device, device_id_type=MESH)

    near = 4 if n_slab >= 32 else 1
    for device in ((s_up, c_up), (s_up, c_dn), (s_dn, c_up), (s_dn, c_dn)):
        hello(device)
    for d in range(1, near + 1):
        hello((lax.rem(s + d, n_slab), c))
        hello((lax.rem(s + n_slab - d, n_slab), c))
    hello((s, c_up))
    hello((s, c_dn))

    loads = [
        pltpu.make_async_copy(a, b, load_sem.at[k])
        for k, (a, b) in enumerate([
            (start_hbm, gath.at[pl.ds(0, 64)]),
            (colsend_hbm, colsend),
            (slabsend_hbm, slabsend),
            (cells_hbm, cells),
            (coupling_hbm, coupling_ref),
            (scale_hbm, scale_ref),
            (nbr_hbm, nbr),
            (screen_hbm, screen),
            (rhs_hbm, rhs),
            (stack_hbm, stack),
            (sums_hbm, sums),
            (weights_hbm.at[c], weights),
        ])
    ]
    for load in loads:
        load.start()

    sub = lax.broadcasted_iota(I32, (8, 128), 0)
    lane = lax.broadcasted_iota(I32, (8, 128), 1)
    e_low = lax.rem(sub, 4) < 2

    def row8(ref, r, v):
        return jnp.broadcast_to(ref[pl.ds(r, 1), pl.ds(128 * v, 128)], (8, 128))

    for load in loads[:6]:
        load.wait()

    col_index = [row8(colsend, k, 0) for k in range(2)]
    beyond = jnp.full((1, 256 - FSLAB), NB)
    slab_index = [
        [
            row8(slabsend, k, 0),
            jnp.broadcast_to(jnp.concatenate([slabsend[pl.ds(k, 1), pl.ds(128, FSLAB - 128)], beyond], axis=1), (8, 128)),
        ]
        for k in range(2)
    ]

    line_row = jnp.zeros((8, 128), F32)
    for k in range(16):
        line_row = jnp.where(lane == k, coupling_ref[k // 8, k // 4 % 2, k % 4], line_row)
        line_row = jnp.where(lane == 16 + k, scale_ref[k // 8, k // 4 % 2, k % 4], line_row)
    line_own[...] = line_row

    def pick(index, source, spans, empty):
        low, high = index & 127, index >> 7
        got = jnp.full((8, 128), empty)
        for v in spans:
            got = jnp.where(high == v, lanes(source(v), low), got)
        return got

    def faces(k):
        for a in range(4):
            for bh in range(2):
                t = 2 * a + bh
                source = lambda v: gath[pl.ds(8 * t, 8), pl.ds(128 * v, 128)]
                fs[k, a, bh] = source(0 if a < 2 else 3)
                fc[k, a, bh] = pick(col_index[0 if bh == 0 else 1], source, range(4), 0.0)

    faces(0)
    cell_source = lambda v: row8(cells, 0, v)
    for k in range(2):
        info_c[k] = pick(col_index[k], cell_source, range(4), NOWHERE)
        for w in range(2):
            info_s[k, :, pl.ds(128 * w, 128)] = jnp.where(sub == 0, slab_index[k][w], cell_source(3 * k))

    pl.semaphore_wait(barrier, 6 + 2 * near)

    reaches = []
    while near < n_slab // 2:
        reaches.append(near)
        near *= 2

    def tell(k):
        if k < len(reaches):
            for d in (reaches[k], n_slab - reaches[k]):
                pl.semaphore_signal(
                    far_sem.at[k], inc=1, device_id=(lax.rem(s + d, n_slab), c), device_id_type=MESH
                )

    def hear(k):
        if k < len(reaches):
            pl.semaphore_wait(far_sem.at[k], 2)

    across_far = n_col > 4

    tell(0)

    def send(src, dst, sent, recv, device):
        copy = pltpu.make_async_remote_copy(
            src_ref=src, dst_ref=dst, send_sem=sent, recv_sem=recv, device_id=device, device_id_type=MESH
        )
        copy.start()
        return copy

    low2, high2 = pl.ds(0, 2), pl.ds(2, 2)

    def send_faces(k):
        return [
            send(src, dst, send_sem.at[8 * k + m], halo_sem.at[8 * k + m], device)
            for m, (src, dst, device) in enumerate([
                (fc.at[k, low2, 0], diag.at[k, low2, 0], (s_dn, c_dn)),
                (fc.at[k, low2, 1], diag.at[k, low2, 1], (s_dn, c_up)),
                (fc.at[k, high2, 0], diag.at[k, high2, 0], (s_up, c_dn)),
                (fc.at[k, high2, 1], diag.at[k, high2, 1], (s_up, c_up)),
                (fs.at[k, low2], rs.at[k, low2], (s_dn, c)),
                (fs.at[k, high2], rs.at[k, high2], (s_up, c)),
                (fc.at[k, :, 0], rc.at[k, :, 0], (s, c_dn)),
                (fc.at[k, :, 1], rc.at[k, :, 1], (s, c_up)),
            ])
        ]

    def bytes_of(ref, sem):
        return pltpu.make_async_copy(ref, ref, sem)

    copies = [send_faces(0)]
    infos = [
        send(src, dst, send_sem.at[16 + m], info_sem.at[m], device)
        for m, (src, dst, device) in enumerate([
            (info_s.at[0], in_s.at[0], (s_dn, c)),
            (info_s.at[1], in_s.at[1], (s_up, c)),
            (info_c.at[0], in_c.at[0], (s, c_dn)),
            (info_c.at[1], in_c.at[1], (s, c_up)),
            (info_c.at[0], in_d.at[0, 0], (s_dn, c_dn)),
            (info_c.at[1], in_d.at[0, 1], (s_dn, c_up)),
            (info_c.at[0], in_d.at[1, 0], (s_up, c_dn)),
            (info_c.at[1], in_d.at[1, 1], (s_up, c_up)),
        ])
    ]
    for load in loads[6:]:
        load.wait()

    def place(there, at):
        return 128 * jnp.where(there, at, AT_NONE)

    above, below, right, left = s < n_slab - 1, s > 0, c < n_col - 1, c > 0

    def raw_rows(r, v):
        if r < 3:
            return nbr[pl.ds(8 * r, 8), pl.ds(128 * v, 128)]
        index = jnp.full((8, 128), NB)
        for k in range(3):
            index = jnp.where(sub == k, row8(nbr, 24 + k, v), index)
        return index

    def place_col(index):
        at = index - COL0
        got = jnp.where(index < NB, index, 128 * AT_NONE)
        got = jnp.where((at >> 7) == 0, place(left, AT_CL) + (at & 127), got)
        return jnp.where((at >> 7) == 1, place(right, AT_CH) + (at & 127), got)

    def place_slab(index, got, up):
        at = index - (SLAB_HIGH if up else SLAB_LOW)
        side, there = (0, above) if up else (1, below)
        listed = jnp.full((8, 128), NB)
        for w in range(2):
            table = jnp.broadcast_to(in_s[side, pl.ds(0, 1), pl.ds(128 * w, 128)], (8, 128))
            listed = jnp.where((at >> 7) == w, lanes(table, at & 127), listed)
        col = listed - COL0
        spot = jnp.where((listed >> 7) == (0 if up else 3), place(there, AT_SLAB) + (listed & 127), 128 * AT_NONE)
        spot = jnp.where((col >> 7) == 0, place(there & left, AT_DL) + (col & 127), spot)
        spot = jnp.where((col >> 7) == 1, place(there & right, AT_DH) + (col & 127), spot)
        return jnp.where((at >= 0) & (at < FSLAB), spot, got)

    def pattern(dx, dy, sz, v):
        o = 9 * (dx + 1) + 3 * (dy + 1) + 1
        if sz == 0:
            return row8(nbn, o, v)
        return jnp.where(e_low, row8(nbn, o + 1, v), row8(nbn, o - 1, v))

    def groups(v):
        for at, blk in enumerate(BLOCKS):
            if blk == 0:
                continue
            sx, sy, sz = blk // 4, blk // 2 % 2, blk % 2
            for dx in ((1, -1) if sx else (0,)):
                for dy in ((1, -1) if sy else (0,)):
                    halves = range(4) if dx == 0 else ((0, 1) if dx == 1 else (2, 3))
                    bhs = (0, 1) if dy == 0 else ((0,) if dy == 1 else (1,))
                    yield at, dx, dy, sz, [2 * a + bh for a in halves for bh in bhs]

    def gather_own():
        for v in range(4):
            for blk, dx, dy, sz, rows in groups(v):
                index = pattern(dx, dy, sz, v)
                low, high = index & 127, index >> 7
                spans = own_sources(v, dx, dy)
                masks = {w: high == w for w in spans}
                for t in rows:
                    got = jnp.zeros((8, 128), F32)
                    for w in spans:
                        got = jnp.where(masks[w], lanes(gath[pl.ds(8 * t, 8), pl.ds(128 * w, 128)], low), got)
                    gath[pl.ds(64 * blk + 8 * t, 8), pl.ds(128 * v, 128)] = got

    def gather_rims(k, v, slot, half, along):
        for blk, dx, dy, sz, rows in groups(v):
            if along and not ((dx == 1 and v == 3) or (dx == -1 and v == 0)):
                continue
            if dy == 0 and not along:
                continue
            index = pattern(dx, dy, sz, v)
            low, high = index & 127, index >> 7
            for t in rows:
                a, bh = t // 2, t % 2
                at = (half, pl.ds(64 * (blk - 2) + 8 * t, 8), pl.ds(128 * slot, 128))
                got = edge[at] if along and dy else jnp.zeros((8, 128), F32)
                if along:
                    got = jnp.where(high == AT_SLAB, lanes(rs[k, a, bh], low), got)
                    if dy:
                        got = jnp.where(high == (AT_DH if dy == 1 else AT_DL), lanes(diag[k, a, bh], low), got)
                else:
                    got = jnp.where(high == (AT_CH if dy == 1 else AT_CL), lanes(rc[k, a, bh], low), got)
                edge[at] = got

    def product(source, rows):
        high, low = split(source)
        both = jnp.dot(stack[:, rows], high, preferred_element_type=F32)
        return both[:64] + both[64:] + jnp.dot(stack[pl.ds(0, 64), rows], low, preferred_element_type=F32)

    def sweep_own():
        gather_own()
        field = gath[pl.ds(0, 64)]
        total = product(gath[...], pl.ds(0, 512))
        base[...] = field + step[...] * (rhs[...] - total - screen[...] * field)

    def finish(half, vs):
        first = 256 if half == 0 else 128
        total = product(edge[half, pl.ds(first - 128, 512 - first)], pl.ds(first, 512 - first))
        for slot, v in enumerate(vs):
            at = pl.ds(128 * v, 128)
            gath[pl.ds(0, 64), at] = base[:, at] - step[:, at] * total[:, 128 * slot : 128 * slot + 128]

    def sweep_rims(k, meanwhile):
        for copy in copies[k][6:]:
            copy.wait_recv()
        for slot, v in enumerate((1, 2)):
            gather_rims(k, v, slot, 0, False)
        finish(0, (1, 2))
        for slot, v in enumerate((0, 3)):
            gather_rims(k, v, slot, 1, False)
        meanwhile()
        for copy in copies[k][:6]:
            copy.wait_recv()
        for slot, v in enumerate((0, 3)):
            gather_rims(k, v, slot, 1, True)
        finish(1, (0, 3))

    step[...] = RELAX / (centre + screen[...])
    edge[1, pl.ds(0, 128)] = jnp.zeros((128, 256), F32)
    for r in range(4):
        for v in range(4):
            nbn[pl.ds(8 * r, 8), pl.ds(128 * v, 128)] = place_col(raw_rows(r, v))
    sweep_own()

    def after_first():
        hear(0)
        tell(1)
        if across_far:
            for d in (2, n_col - 2):
                pl.semaphore_signal(far_sem.at[3], inc=1, device_id=(s, lax.rem(c + d, n_col)), device_id_type=MESH)
        for copy in infos[:2]:
            copy.wait_recv()
        for r in range(4):
            at = (pl.ds(8 * r, 8), pl.ds(0 if r < 2 else 384, 128))
            nbn[at] = place_slab(raw_rows(r, 0 if r < 2 else 3), nbn[at], r >= 2)

    reach = {
        (0, 0): ((0, 1, 2, 3), range(4)),
        (0, -1): ((0, 1, 2), range(4)),
        (0, 1): ((0, 1, 2, 3), range(4)),
        (-1, 0): ((0, 1), (0,)),
        (-1, -1): ((0,), (0,)),
        (-1, 1): ((0, 1), (0,)),
        (1, 0): ((2, 3), (3,)),
        (1, -1): ((2,), (3,)),
        (1, 1): ((3,), (3,)),
    }
    nought = jnp.zeros((8, 128), F32)
    held = {(block, k): nought for block in reach for k in range(16)}

    def give(vs):
        found = {}
        for v in vs:
            at = pl.ds(128 * v, 128)
            field = gath[pl.ds(0, 64), at]
            high, low = split(field)
            both = jnp.dot(sums[...], high, preferred_element_type=F32)
            given = both[:32] + both[32:] + jnp.dot(sums[pl.ds(0, 32)], low, preferred_element_type=F32)
            local = jnp.sum(rhs[:, at] - screen[:, at] * field, axis=0, keepdims=True)
            row_at = lax.broadcasted_iota(I32, (32, 128), 0)
            found[v] = (jnp.where(row_at == 13, jnp.broadcast_to(local, (32, 128)), 0.0) - given) * (1.0 / 64.0)
        return found

    def tally(found):
        for (ds, dc), (rs_of, vs_of) in reach.items():
            for k in range(16):
                for v in vs_of:
                    if v in found:
                        for r in rs_of:
                            hit = codes[pl.ds(8 * r, 8), pl.ds(128 * v, 128)] == 48 * (ds + 1) + 16 * (dc + 1) + k
                            part = jnp.where(hit, found[v][8 * r : 8 * r + 8], 0.0)
                            held[(ds, dc), k] = held[(ds, dc), k] + part

    def after_second():
        hear(1)
        tell(2)
        tally(give((1, 2)))

    sweep_rims(0, after_first)
    faces(1)
    copies.append(send_faces(1))
    sweep_own()

    for copy in infos[2:]:
        copy.wait_recv()
    own_codes = [row8(cells, 0, v) + 64 for v in range(4)]
    col_codes = [in_c[1] + 48, in_c[0] + 80]
    for r in range(4):
        for v in range(4):
            index = nbn[pl.ds(8 * r, 8), pl.ds(128 * v, 128)]
            low, high = index & 127, index >> 7
            code = jnp.full((8, 128), NOWHERE)
            for w in range(4):
                code = jnp.where(high == w, lanes(own_codes[w], low), code)
            for w, at in enumerate((AT_CL, AT_CH)):
                code = jnp.where(high == at, lanes(col_codes[w], low), code)
            if (r < 2 and v == 0) or (r >= 2 and v == 3):
                side, first = (1, 0) if r < 2 else (0, 96)
                beside = jnp.broadcast_to(in_s[side, pl.ds(1, 1), pl.ds(0, 128)], (8, 128))
                code = jnp.where(high == AT_SLAB, lanes(beside, low) + first + 16, code)
                code = jnp.where(high == AT_DL, lanes(in_d[side, 1], low) + first, code)
                code = jnp.where(high == AT_DH, lanes(in_d[side, 0], low) + first + 32, code)
            codes[pl.ds(8 * r, 8), pl.ds(128 * v, 128)] = code

    sweep_rims(1, after_second)
    tally(give((0, 3)))

    def fold(parts):
        for bit in (4, 2, 1):
            keep = (sub & bit) == 0
            merged = []
            for k in range(bit):
                one, two = parts[k], parts[k + bit]
                stay, go = jnp.where(keep, one, two), jnp.where(keep, two, one)
                if bit == 4:
                    merged.append(stay + pltpu.roll(go, 4, 0))
                else:
                    merged.append(stay + jnp.where(keep, pltpu.roll(go, 8 - bit, 0), pltpu.roll(go, bit, 0)))
            parts = merged
        return parts[0]

    stacked = []
    for dc in (-1, 0, 1):
        plain, swapped = [], []
        for ds in (-1, 0, 1):
            for x in range(2):
                parts = [held[(ds, dc), 8 * x + k] for k in range(8)]
                total = fold(parts)
                plain.append(total)
                swapped.append(pltpu.roll(total, 4, 0))
        stacked += plain + [nought, nought] + swapped + [nought, nought]
    high, low = split(jnp.concatenate(stacked, axis=0))
    ones = jnp.ones((16, 128), BF16)
    across = (((1,), (1,)), ((), ()))
    summed = lax.dot_general(ones, high, across, preferred_element_type=F32) + lax.dot_general(
        ones, low, across, preferred_element_type=F32
    )
    message = jnp.where(
        sub == 0, summed[:8, :128], jnp.where(sub == 1, summed[:8, 128:256], jnp.where(sub == 2, summed[:8, 256:], 0.0))
    )
    if across_far:
        pl.semaphore_wait(far_sem.at[3], 2)
    mix_own[...] = message
    mix_all[pl.ds(c, 1)] = message.reshape(1, 8, 128)

    @pl.loop(1, n_col)
    def _(d):
        send(mix_own, mix_all.at[c], send_sem.at[25], mix_sem, (s, lax.rem(c + d, n_col)))

    hear(2)
    line_all[pl.ds(s, 1)] = line_own[pl.ds(0, 1)].reshape(1, 1, 128)

    @pl.loop(1, n_slab)
    def _(d):
        send(line_own.at[pl.ds(0, 1)], line_all.at[s], send_sem.at[24], line_sem, (lax.rem(s + d, n_slab), c))

    bytes_of(mix_all.at[pl.ds(0, n_col - 1)], mix_sem).wait()
    mixed = jnp.zeros((8, 128), F32)
    for k in range(n_col):
        mixed = mixed + weights[k] * mix_all[k]
    row = jnp.sum(mixed, axis=0, keepdims=True)
    row = row + pltpu.roll(row, 64, 1)
    row_own[...] = row
    row_all[pl.ds(s, 1)] = row.reshape(1, 1, 128)

    @pl.loop(1, n_slab, unroll=9 if n_slab == 64 else 1)
    def _(d):
        send(row_own, row_all.at[s], send_sem.at[26], row_sem, (lax.rem(s + d, n_slab), c))

    bytes_of(line_all.at[pl.ds(0, n_slab - 1)], line_sem).wait()
    all_rows = line_all[...].reshape(n_slab, 128)
    big_lane = lax.broadcasted_iota(I32, (n_slab, 128), 1)
    big_row = lax.broadcasted_iota(I32, (n_slab, 128), 0)
    spot = big_lane & 7
    c0, c1, p0, p1 = [lanes(all_rows, spot + 8 * k) for k in range(4)]
    first = big_lane < 64
    after, here = big_row > s, big_row == s

    def rows_down(x, d, fill):
        return jnp.where(big_row >= d, pltpu.roll(x, d, 0), fill)

    def rows_up(x, d, fill):
        return jnp.where(big_row < n_slab - d, pltpu.roll(x, n_slab - d, 0), fill)

    run = jnp.where(after, c0 * c1, jnp.where(here, jnp.where(first, c0 * c1, c1), 1.0))
    d = 1
    while d < n_slab:
        run = run * rows_down(run, d, 1.0)
        d *= 2
    run = rows_down(run, 1, 1.0)
    w0 = jnp.where(after, run, jnp.where(here & first, 1.0, 0.0))
    w1 = jnp.where(after, run * c0, jnp.where(here, jnp.where(first, c0, 1.0), 0.0))
    u0, u1 = p0 * w0, p1 * w1
    c0_next = rows_up(c0, 1, 0.0)
    tail, factor = u0 + c1 * u1, c1 * c0_next
    d = 1
    while d < n_slab:
        tail = tail + factor * rows_up(tail, d, 0.0)
        factor = factor * rows_up(factor, d, 0.0)
        d *= 2
    second = u1 + c0_next * rows_up(tail, 1, 0.0)
    give = jnp.where((big_lane & 8) == 0, tail, second)
    part = (big_lane & 63) >> 4
    line_w[...] = jnp.where(
        part == 0, rows_down(give, 1, 0.0), jnp.where(part == 1, give, jnp.where(part == 2, rows_up(give, 1, 0.0), 0.0))
    )

    bytes_of(row_all.at[pl.ds(0, n_slab - 1)], row_sem).wait()
    corr = jnp.sum(line_w[...] * row_all[...].reshape(n_slab, 128), axis=0, keepdims=True)
    corr = corr + pltpu.roll(corr, 128 - 8, 1)
    corr = corr + pltpu.roll(corr, 128 - 16, 1) + pltpu.roll(corr, 128 - 32, 1)
    corr = jnp.broadcast_to(corr, (8, 128))
    results = []
    for v in range(4):
        cell = row8(cells, 0, v)
        lift = lanes(corr, (cell >> 3) * 64 + (cell & 7))
        at = pl.ds(128 * v, 128)
        for t in range(8):
            base[pl.ds(8 * t, 8), at] = gath[pl.ds(8 * t, 8), at] + lift
        results.append(pltpu.make_async_copy(base.at[:, at], out_hbm.at[:, at], out_sem.at[v]))
        results[v].start()

    for copy in copies[0] + copies[1] + infos:
        copy.wait_send()
    bytes_of(line_all.at[pl.ds(0, n_slab - 1)], send_sem.at[24]).wait()
    bytes_of(mix_all.at[pl.ds(0, n_col - 1)], send_sem.at[25]).wait()
    bytes_of(row_all.at[pl.ds(0, n_slab - 1)], send_sem.at[26]).wait()
    for result in results:
        result.wait()


def solution(mesh):
    n_slab, n_col = mesh.shape["slab"], mesh.shape["col"]
    stack, sums, weights, centre = tables(n_col)

    def shards(rhs, start, screen, neighbours, col_send, slab_send, coarse_map, coupling, coarse_scale):
        hbm = pl.BlockSpec(memory_space=pltpu.HBM)
        vmem = pltpu.VMEM
        dma = pltpu.SemaphoreType.DMA
        return pl.pallas_call(
            functools.partial(kernel, n_slab, n_col, centre),
            out_shape=jax.ShapeDtypeStruct((64, NB), F32),
            in_specs=[hbm] * 12,
            out_specs=hbm,
            scratch_shapes=[
                vmem((64, NB), F32),
                vmem((64, NB), F32),
                vmem((64, NB), F32),
                vmem((27, NB), I32),
                vmem((2, FCOL), I32),
                vmem((2, FSLAB), I32),
                vmem((1, NB), I32),
                pltpu.SMEM((2, 2, 4), F32),
                pltpu.SMEM((2, 2, 4), F32),
                vmem((128, 512), BF16),
                vmem((64, 64), BF16),
                vmem((n_col, 8, 128), F32),
                vmem((512, NB), F32),
                vmem((2, 384, 256), F32),
                vmem((64, NB), F32),
                vmem((32, NB), I32),
                vmem((2, 4, 2, 8, 128), F32),
                vmem((2, 4, 2, 8, 128), F32),
                vmem((2, 4, 2, 8, 128), F32),
                vmem((2, 4, 2, 8, 128), F32),
                vmem((2, 4, 2, 8, 128), F32),
                vmem((2, 8, 256), I32),
                vmem((2, 8, 128), I32),
                vmem((2, 8, 256), I32),
                vmem((2, 8, 128), I32),
                vmem((2, 2, 8, 128), I32),
                vmem((32, NB), I32),
                vmem((8, 128), F32),
                vmem((n_slab, 1, 128), F32),
                vmem((n_slab, 128), F32),
                vmem((n_col, 8, 128), F32),
                vmem((8, 128), F32),
                vmem((1, 128), F32),
                vmem((n_slab, 1, 128), F32),
                dma((12,)),
                dma((4,)),
                dma((27,)),
                dma((16,)),
                dma((8,)),
                dma,
                dma,
                dma,
                pltpu.SemaphoreType.REGULAR((4,)),
            ],
            compiler_params=pltpu.CompilerParams(
                collective_id=0, has_side_effects=True, vmem_limit_bytes=63 * 1024 * 1024
            ),
            cost_estimate=pl.CostEstimate(flops=10**8, bytes_accessed=10**6, transcendentals=0),
        )(
            rhs, start, screen, neighbours, col_send, slab_send,
            coarse_map.reshape(1, NB), coupling, coarse_scale,
            jnp.asarray(stack), jnp.asarray(sums), jnp.asarray(weights),
        )

    block = P(None, ("slab", "col"))
    line = P("slab", "col", None)
    placed = (block,) * 6 + (P(("slab", "col")), line, line)
    return jax.shard_map(shards, mesh=mesh, in_specs=placed, out_specs=block, check_vma=False)
```
